32 devices in a mesh: gy: 8 (over z, y), gz: 4 (over x, core).
Axes of the slice: x: 2, y: 2, z: 4, core: 2. Of those that a mesh axis runs over, the one named last changes fastest.
Arguments:
- field: bfloat16 [32, 8, 128, 1024], P(None, None, 'gy', 'gz'), may hold values from -6 to 6
- spectral_weight: bfloat16 [256, 32, 1024], P('gy', 'gz'), may hold values from -1 to 1
- point_weight: bfloat16 [32, 32], replicated, may hold values from -1 to 1
- bias: float32 [32], replicated, may hold values from -3 to 3
Outputs:
- layer_out: bfloat16 [32, 8, 128, 1024], P(None, None, 'gy', 'gz')
The draws below stay inside these ranges and needn't reach their ends.
All inputs are finite; a program needn't handle non-finite values.
Results may differ from the reference program's by a relative error of at most 0.013.
Values may be sent and summed in bfloat16 or wider, within the bound.
A program may use at most 64 MiB of HBM per device.

```python
import math
import jax
import jax.numpy as jnp
from jax import lax

C = 32
KY = 32
KZ = 32
X = 8
KX = 8
NY = 128
NZ = 1024


def steps_of(own_key, dims, split, least, high):
    loudness = 1.0
    for axis_at, blocks in split:
        heights = jax.random.uniform(jax.random.fold_in(jax.random.fold_in(own_key, 6), axis_at), (blocks,), jnp.float32, least / len(split), high / len(split))
        loudness = loudness * jnp.repeat(jnp.exp(heights), dims[axis_at] // blocks).reshape((-1,) + (1,) * (len(dims) - 1 - axis_at))
    return loudness


def normal_values(key, shape, spread, most, pieces=(), held_as=jnp.bfloat16):
    level = steps_of(key, shape, pieces, -0.22, 0.18) if pieces else 1.0
    entries = jax.random.normal(key, shape, jnp.float32) * spread * level
    return jnp.minimum(jnp.maximum(entries, -most), most).astype(held_as)


def setup_inputs(seed: int = 0) -> dict:
    arg_keys = jax.random.split(jax.random.key(seed), 5)
    return {
        "field": normal_values(arg_keys[0], (C, X, NY, NZ), 1.0, 6.0, ((2, 8), (3, 4))),
        "spectral_weight": normal_values(arg_keys[1], (KX * KY, KZ, C * C), C ** -0.5, 1.0, ((0, 8), (1, 4))),
        "point_weight": normal_values(arg_keys[2], (C, C), C ** -0.5, 1.0),
        "bias": normal_values(arg_keys[3], (C,), 0.5, 3.0, (), jnp.float32),
    }


def basis(count, length, start, size, norm):
    modes = jnp.arange(count, dtype=jnp.float32)[:, None]
    spots = (start + lax.iota(jnp.int32, size)).astype(jnp.float32)[None, :]
    value = norm * jnp.cos(jnp.pi * modes * (spots + 0.5) / length)
    return jnp.where(modes == 0, value * math.sqrt(0.5), value)

def reference(field, spectral_weight, point_weight, bias):
    highest = lax.Precision.HIGHEST
    block = math.gcd(NY, 64)
    indices = jnp.arange(NY // block, dtype=jnp.int32)
    rounded_z = basis(KZ, NZ, 0, NZ, math.sqrt(2.0 / NZ)).astype(jnp.bfloat16)
    analysis_z = lax.optimization_barrier(rounded_z).astype(jnp.float32)
    analysis_y = basis(KY, NY, 0, NY, math.sqrt(2.0 / NY))
    analysis_x = basis(KX, X, 0, X, math.sqrt(2.0 / X))

    def forward(carry, index):
        piece = lax.dynamic_slice_in_dim(field, index * block, block, 2).astype(jnp.float32)
        part = jnp.einsum('cxyz,kz->cxyk', piece, analysis_z, precision=highest)
        rows_basis = lax.dynamic_slice_in_dim(analysis_y, index * block, block, 1)
        return (carry + jnp.einsum('cxyk,jy->cxjk', part, rows_basis, precision=highest), None)
    start = jnp.zeros((C, X, KY, KZ), jnp.float32)
    summed, unused = lax.scan(forward, start, indices)
    spectrum = jnp.einsum('cxjk,ix->cijk', summed, analysis_x, precision=highest)
    weight = spectral_weight.astype(jnp.float32).reshape(KX, KY, KZ, C, C)
    mixed = jnp.einsum('cijk,ijkco->oijk', spectrum, weight, precision=highest).astype(jnp.bfloat16)
    mixed = lax.optimization_barrier(mixed).astype(jnp.float32)
    synth_x = basis(KX, X, 0, X, math.sqrt(2.0 / KX))
    synth_y = basis(KY, NY, 0, NY, math.sqrt(2.0 / KY))
    synth_z = basis(KZ, NZ, 0, NZ, math.sqrt(2.0 / KZ))
    modes_x = jnp.einsum('cijk,ix->cxjk', mixed, synth_x, precision=highest)
    point = point_weight.astype(jnp.float32)
    shift = bias.astype(jnp.float32)[:, None, None, None]

    def backward(index):
        piece = lax.dynamic_slice_in_dim(field, index * block, block, 2).astype(jnp.float32)
        rows_basis = lax.dynamic_slice_in_dim(synth_y, index * block, block, 1)
        spatial = jnp.einsum('cxjk,jy->cxyk', modes_x, rows_basis, precision=highest)
        spatial = jnp.einsum('cxyk,kz->cxyz', spatial, synth_z, precision=highest)
        local = jnp.einsum('cxyz,co->oxyz', piece, point, precision=highest)
        return jax.nn.gelu(spatial + local + shift, approximate=True).astype(jnp.bfloat16)
    blocks = lax.map(backward, indices)
    return jnp.moveaxis(blocks, 0, 2).reshape(C, X, NY, NZ)
```

```python
import functools
import math

import jax
import jax.numpy as jnp
import ml_dtypes
import numpy as np
from jax import lax
from jax.experimental import pallas as pl
from jax.experimental.pallas import tpu as pltpu
from jax.sharding import PartitionSpec as P

KY = 32
KZ = 32
BF16 = jnp.bfloat16
F32 = jnp.float32
MESH = pl.DeviceIdType.MESH
SHARE = 8
HALF = 256


def basis(count, length, norm):
    modes = np.arange(count)[:, None]
    spots = np.arange(length)[None, :]
    value = norm * np.cos(np.pi * modes * (spots + 0.5) / length)
    return np.where(modes == 0, value * math.sqrt(0.5), value)


def tables(n_y, n_z, planes, rows, depth, first_share):
    total_rows, total_depth = rows * n_y, depth * n_z
    az = basis(KZ, total_depth, math.sqrt(2.0 / total_depth))
    az = az.astype(np.float32).astype(ml_dtypes.bfloat16).astype(np.float64)
    ax = basis(planes, planes, math.sqrt(2.0 / planes))
    sz = basis(KZ, total_depth, math.sqrt(2.0 / KZ))

    def joint(x_basis, z_basis):
        z = z_basis.reshape(n_z, SHARE, n_z, depth)
        both = np.einsum("ix,bkdz->dxbikz", x_basis, z)
        return both.reshape(n_z, planes, planes * KZ, depth).astype(ml_dtypes.bfloat16)

    ay = basis(KY, total_rows, math.sqrt(2.0 / total_rows))
    sy = basis(KY, total_rows, math.sqrt(2.0 / KY))
    blocks = KY // first_share

    def lanes(y_basis):
        parts = y_basis.reshape(blocks, first_share, n_y, rows)
        return np.tile(parts, (1, 1, 1, HALF // rows)).astype(np.float32)

    analysis_y = lanes(ay)
    synth_y = np.ascontiguousarray(np.swapaxes(lanes(sy), 1, 2))
    return joint(ax, az), joint(ax, sz), analysis_y, synth_y


def select(rows, columns, row_of, column_of):
    r = lax.broadcasted_iota(jnp.int32, (rows, columns), 0)
    c = lax.broadcasted_iota(jnp.int32, (rows, columns), 1)
    return jnp.where(row_of(r) == column_of(c), 1.0, 0.0).astype(F32)


def spectral_kernel(
    n_y, n_z, field, a_tab, weight, point, ay_tab, sy_tab, gt_out, kron_out,
    f_v, a_v, w_v, ay_v, sy_v, e1, e2, part, got1, owned, got2, u_v, m_v, tout, got3, modes,
    load_sem, send1, recv1, send2, recv2, send3, recv3, send4, recv4,
):
    me_y, me_z = lax.axis_index("gy"), lax.axis_index("gz")
    planes = f_v.shape[1]
    chans = f_v.shape[0]
    rows = f_v.shape[2]
    group = n_y // planes
    first_share = w_v.shape[0]
    mine, place = lax.div(me_y, group), lax.rem(me_y, group)
    block = place if first_share < KY else 0
    others = [(d, t) for d in range(planes) for t in range(group)][1:]

    def at(d, t):
        return lax.rem(mine + d, planes) * group + lax.rem(place + t, group)

    def came(d, t):
        return lax.rem(mine - d + planes, planes) * group + lax.rem(place - t + group, group)

    def peer(e):
        return lax.rem(me_z + e, n_z)

    barrier = pltpu.get_barrier_semaphore()
    for e in range(1, n_z):
        pl.semaphore_signal(
            barrier, inc=1, device_id=(me_y, peer(e)), device_id_type=MESH
        )
    for d, t in others:
        pl.semaphore_signal(
            barrier, inc=1, device_id=(at(d, t), me_z), device_id_type=MESH
        )

    half = chans // 2
    loads = [
        pltpu.make_async_copy(field.at[0:half], f_v.at[0:half], load_sem.at[0]),
        pltpu.make_async_copy(a_tab.at[me_z], a_v, load_sem.at[1]),
        pltpu.make_async_copy(field.at[half:chans], f_v.at[half:chans], load_sem.at[2]),
        pltpu.make_async_copy(weight, w_v, load_sem.at[3]),
        pltpu.make_async_copy(ay_tab.at[block], ay_v, load_sem.at[4]),
        pltpu.make_async_copy(sy_tab.at[block], sy_v, load_sem.at[5]),
    ]
    for load in loads:
        load.start()

    halves = []
    loads[1].wait()
    for h in range(2):
        loads[2 * h].wait()
        total = jnp.zeros((planes * KZ, HALF), F32)
        for x in range(planes):
            grid = f_v[h * half:(h + 1) * half, x].reshape(HALF, f_v.shape[3])
            total += lax.dot_general(
                a_v[x], grid, (((1,), (1,)), ((), ())), preferred_element_type=F32
            )
        halves.append(total.reshape(planes * n_z, SHARE, HALF))
    part[...] = jnp.concatenate(halves, axis=1).astype(BF16)

    pl.semaphore_wait(barrier, n_z - 1 + len(others))

    started = []
    order = list(range(1, planes)) + [0]
    first = {}
    for d in order:
        i = lax.rem(mine + d, planes)
        for e in range(1, n_z):
            copy = pltpu.make_async_remote_copy(
                src_ref=part.at[peer(e) * planes + i],
                dst_ref=got1.at[e - 1, i],
                send_sem=send1.at[e - 1, d],
                recv_sem=recv1.at[e - 1, d],
                device_id=(me_y, peer(e)),
                device_id_type=MESH,
            )
            copy.start()
            first[e, d] = copy
            started.append(copy)

    e1[...] = select(*e1.shape, lambda r: r // rows, lambda c: c // chans).astype(BF16)
    e2[...] = select(*e2.shape, lambda r: r % chans, lambda c: c // rows).astype(BF16)

    second = {}
    for d in order:
        i = lax.rem(mine + d, planes)
        total = part[me_z * planes + i].astype(F32)
        for e in range(1, n_z):
            first[e, d].wait_recv()
            total += got1[e - 1, i].astype(F32)
        owned[i] = total.astype(BF16)
        for t in range(group):
            if d == 0 and t == 0:
                got2[me_y] = total.astype(BF16)
                continue
            copy = pltpu.make_async_remote_copy(
                src_ref=owned.at[i],
                dst_ref=got2.at[me_y],
                send_sem=send2.at[d * group + t],
                recv_sem=recv2.at[d * group + t],
                device_id=(at(d, t), me_z),
                device_id_type=MESH,
            )
            copy.start()
            second[d, t] = copy
            started.append(copy)

    spread = select(chans * rows, chans, lambda r: r // rows, lambda c: c).astype(BF16)
    wide = lax.dot_general(
        spread, point[...], (((1,), (1,)), ((), ())), preferred_element_type=F32
    ).astype(BF16)
    wide = lax.dot_general(
        wide, spread, (((1,), (1,)), ((), ())), preferred_element_type=F32
    )
    same = select(*wide.shape, lambda r: r % rows, lambda c: c % rows)
    kron_out[...] = (wide * same).astype(BF16)

    for load in loads[3:]:
        load.wait()
    for d, t in others:
        second[d, t].wait_recv()
    for h in range(2):
        pieces = [got2[s].astype(F32)[h * SHARE:(h + 1) * SHARE] for s in range(n_y)]
        for j in range(first_share):
            total = pieces[0] * ay_v[j, 0:1, :]
            for s in range(1, n_y):
                total += pieces[s] * ay_v[j, s:s + 1, :]
            u_v[j, :, h * HALF:(h + 1) * HALF] = total

    mode_rows = first_share * SHARE
    spectrum = jnp.dot(
        u_v[...].reshape(mode_rows, 2 * HALF).astype(BF16), e1[...], preferred_element_type=F32
    )
    terms = spectrum * w_v[...].astype(F32).reshape(mode_rows, chans * chans)
    mixed = jnp.dot(terms.astype(BF16), e2[...], preferred_element_type=F32)
    m_v[...] = mixed.reshape(first_share, SHARE, 2 * HALF)

    third = {}
    for d, t in others + [(0, 0)]:
        target = at(d, t)
        synth = sy_v[target]
        sides = []
        for h in range(2):
            total = m_v[0, :, h * HALF:(h + 1) * HALF] * synth[0:1, :]
            for j in range(1, first_share):
                total += m_v[j, :, h * HALF:(h + 1) * HALF] * synth[j:j + 1, :]
            sides.append(total)
        value = jnp.concatenate(sides, axis=0).astype(BF16)
        if d == 0 and t == 0:
            got3[me_y] = value
            continue
        tout[target] = value
        copy = pltpu.make_async_remote_copy(
            src_ref=tout.at[target],
            dst_ref=got3.at[me_y],
            send_sem=send3.at[d * group + t],
            recv_sem=recv3.at[d * group + t],
            device_id=(target, me_z),
            device_id_type=MESH,
        )
        copy.start()
        third[d, t] = copy
        started.append(copy)

    fourth = []
    for d in range(planes):
        i = lax.rem(mine - d + planes, planes)
        total = None
        for t in range(group):
            if (d, t) != (0, 0):
                third[d, t].wait_recv()
            piece = got3[came(d, t)]
            if group > 1:
                piece = piece.astype(F32)
            total = piece if total is None else total + piece
        slot = me_z * planes + i
        modes[slot] = total.astype(BF16)
        for e in range(1, n_z):
            copy = pltpu.make_async_remote_copy(
                src_ref=modes.at[slot],
                dst_ref=modes.at[slot],
                send_sem=send4.at[e - 1, d],
                recv_sem=recv4.at[e - 1, d],
                device_id=(me_y, peer(e)),
                device_id_type=MESH,
            )
            copy.start()
            fourth.append(copy)
    for copy in fourth:
        copy.wait_recv()
    for h in range(2):
        value = modes[...].astype(F32)[:, h * SHARE:(h + 1) * SHARE, :]
        value = value.reshape(planes * KZ, HALF)
        gt_out[h * HALF:(h + 1) * HALF, :] = value.T.astype(BF16)
    for copy in started + fourth:
        copy.wait_send()


def grid_kernel(
    field, b_tab, bias, gt, kron, out, f_v, b_v, bias_v, o_v, field_sem, basis_sem, out_sem
):
    me_z = lax.axis_index("gz")
    chans, planes, rows, depth = f_v.shape
    loads = []
    for x in range(planes):
        one = pltpu.make_async_copy(field.at[:, x], f_v.at[:, x], field_sem.at[x])
        two = pltpu.make_async_copy(b_tab.at[me_z, x], b_v.at[x], basis_sem.at[x])
        one.start()
        two.start()
        loads.append((one, two))
    for o in range(chans):
        bias_v[o * rows:(o + 1) * rows, :] = jnp.full((rows, depth), bias[o], F32)
    stores = []
    scale = math.sqrt(2.0 / math.pi)
    for x in range(planes):
        for load in loads[x]:
            load.wait()
        grid = f_v[:, x].reshape(chans * rows, depth)
        value = jnp.dot(kron[...], grid, preferred_element_type=F32)
        value += jnp.dot(gt[...], b_v[x], preferred_element_type=F32)
        value += bias_v[...]
        inner = value * (scale + (scale * 0.044715) * (value * value))
        small = 0.5 * value
        value = small + small * jnp.tanh(inner)
        o_v[:, x] = value.astype(BF16).reshape(chans, rows, depth)
        store = pltpu.make_async_copy(o_v.at[:, x], out.at[:, x], out_sem.at[x])
        store.start()
        stores.append(store)
    for store in stores:
        store.wait()


def shards(n_y, n_z, field, spectral_weight, point_weight, bias):
    chans, planes, rows, depth = field.shape
    first_share, depth_share = spectral_weight.shape[:2]
    assert depth_share == SHARE and chans * rows == 2 * HALF and first_share <= KY
    assert n_y % planes == 0 and depth_share * n_z == KZ
    a_tab, b_tab, ay_tab, sy_tab = tables(n_y, n_z, planes, rows, depth, first_share)
    group = n_y // planes
    vmem = pl.BlockSpec(memory_space=pltpu.VMEM)
    any_ = pl.BlockSpec(memory_space=pl.ANY)
    wide = 2 * HALF
    dma = pltpu.SemaphoreType.DMA
    gt, kron = pl.pallas_call(
        functools.partial(spectral_kernel, n_y, n_z),
        out_shape=(
            jax.ShapeDtypeStruct((wide, planes * KZ), BF16),
            jax.ShapeDtypeStruct((wide, wide), BF16),
        ),
        in_specs=[any_, any_, any_, vmem, any_, any_],
        out_specs=(vmem, vmem),
        scratch_shapes=[
            pltpu.VMEM(field.shape, BF16),
            pltpu.VMEM(a_tab.shape[1:], BF16),
            pltpu.VMEM(spectral_weight.shape, BF16),
            pltpu.VMEM(ay_tab.shape[1:], F32),
            pltpu.VMEM(sy_tab.shape[1:], F32),
            pltpu.VMEM((wide, chans * chans), BF16),
            pltpu.VMEM((chans * chans, wide), BF16),
            pltpu.VMEM((n_z * planes, 16, HALF), BF16),
            pltpu.VMEM((n_z - 1, planes, 16, HALF), BF16),
            pltpu.VMEM((planes, 16, HALF), BF16),
            pltpu.VMEM((n_y, 16, HALF), BF16),
            pltpu.VMEM((first_share, SHARE, wide), F32),
            pltpu.VMEM((first_share, SHARE, wide), F32),
            pltpu.VMEM((n_y, 16, HALF), BF16),
            pltpu.VMEM((n_y, 16, HALF), BF16),
            pltpu.VMEM((n_z * planes, 16, HALF), BF16),
            dma((6,)),
            dma((n_z - 1, planes)),
            dma((n_z - 1, planes)),
            dma((n_y,)),
            dma((n_y,)),
            dma((n_y,)),
            dma((n_y,)),
            dma((n_z - 1, planes)),
            dma((n_z - 1, planes)),
        ],
        compiler_params=pltpu.CompilerParams(
            collective_id=0, has_side_effects=True, vmem_limit_bytes=40 * 1024 * 1024
        ),
        name="spectral",
    )(field, a_tab, spectral_weight, point_weight, ay_tab, sy_tab)
    return pl.pallas_call(
        grid_kernel,
        out_shape=jax.ShapeDtypeStruct(field.shape, BF16),
        in_specs=[any_, any_, pl.BlockSpec(memory_space=pltpu.SMEM), vmem, vmem],
        out_specs=any_,
        scratch_shapes=[
            pltpu.VMEM(field.shape, BF16),
            pltpu.VMEM(b_tab.shape[1:], BF16),
            pltpu.VMEM((chans * rows, depth), F32),
            pltpu.VMEM(field.shape, BF16),
            dma((planes,)),
            dma((planes,)),
            dma((planes,)),
        ],
        compiler_params=pltpu.CompilerParams(vmem_limit_bytes=40 * 1024 * 1024),
        name="grid",
    )(field, b_tab, bias, gt, kron)


def solution(mesh):
    return jax.shard_map(
        functools.partial(shards, mesh.shape["gy"], mesh.shape["gz"]),
        mesh=mesh,
        in_specs=(P(None, None, "gy", "gz"), P("gy", "gz", None), P(), P()),
        out_specs=P(None, None, "gy", "gz"),
        check_vma=False,
    )
```

```python
import functools
import math

import jax
import jax.numpy as jnp
import ml_dtypes
import numpy as np
from jax import lax
from jax.experimental import pallas as pl
from jax.experimental.pallas import tpu as pltpu
from jax.sharding import PartitionSpec as P

KY = 32
KZ = 32
BF16 = jnp.bfloat16
F32 = jnp.float32
MESH = pl.DeviceIdType.MESH
SHARE = 8
HALF = 256


def basis(count, length, norm):
    modes = np.arange(count)[:, None]
    spots = np.arange(length)[None, :]
    value = norm * np.cos(np.pi * modes * (spots + 0.5) / length)
    return np.where(modes == 0, value * math.sqrt(0.5), value)


def tables(n_y, n_z, planes, rows, depth, first_share):
    total_rows, total_depth = rows * n_y, depth * n_z
    az = basis(KZ, total_depth, math.sqrt(2.0 / total_depth))
    az = az.astype(np.float32).astype(ml_dtypes.bfloat16).astype(np.float64)
    ax = basis(planes, planes, math.sqrt(2.0 / planes))
    sz = basis(KZ, total_depth, math.sqrt(2.0 / KZ))

    def joint(x_basis, z_basis):
        z = z_basis.reshape(n_z, SHARE, n_z, depth)
        both = np.einsum("ix,bkdz->dxbikz", x_basis, z)
        return both.reshape(n_z, planes, planes * KZ, depth).astype(ml_dtypes.bfloat16)

    ay = basis(KY, total_rows, math.sqrt(2.0 / total_rows))
    sy = basis(KY, total_rows, math.sqrt(2.0 / KY))
    blocks = KY // first_share

    def lanes(y_basis):
        parts = y_basis.reshape(blocks, first_share, n_y, rows)
        return np.tile(parts, (1, 1, 1, HALF // rows)).astype(np.float32)

    analysis_y = lanes(ay)
    synth_y = np.ascontiguousarray(np.swapaxes(lanes(sy), 1, 2))
    return joint(ax, az), joint(ax, sz), analysis_y, synth_y


def bits(count):
    assert count & (count - 1) == 0
    return count.bit_length() - 1


def select(shape, row_of, column_of):
    r = row_of(lax.broadcasted_iota(jnp.int32, shape, 0))
    c = column_of(lax.broadcasted_iota(jnp.int32, shape, 1))
    return jnp.where(r == c, 1.0, 0.0).astype(F32)


def spectral_kernel(
    n_y, n_z, field, a_tab, b_tab, weight, point, bias, ay_tab, sy_tab, local, gt_out, b_out,
    f_v, a_v, w_v, p_v, bias_s, bias_v, ay_v, sy_v, e1, e2, spread, kron,
    part, got1, owned, got2, u_v, m_v, tout, got3, modes,
    load_sem, grid_sem, a_sem, send1, recv1, send2, recv2, send3, recv3, send4, recv4,
):
    me_y, me_z = lax.axis_index("gy"), lax.axis_index("gz")
    chans, planes, rows, depth = f_v.shape
    pairs = planes // 2
    group = n_y // planes
    first_share = w_v.shape[0]
    mine, place = lax.div(me_y, group), lax.rem(me_y, group)
    block = place if first_share < KY else 0
    others = [(d, t) for d in range(planes) for t in range(group)][1:]

    def flip(index, mask):
        for k in range(bits(planes)):
            if mask >> k & 1:
                bit = lax.rem(lax.div(index, 1 << k), 2)
                index = index + (1 << k) * (1 - 2 * bit)
        return index

    def at(d, t):
        return flip(mine, d) * group + lax.rem(place + t, group)

    def came(d, t):
        return flip(mine, d) * group + lax.rem(place - t + group, group)

    def peer(e):
        return lax.rem(me_z + e, n_z)

    barrier = pltpu.get_barrier_semaphore()
    for e in range(1, n_z):
        pl.semaphore_signal(
            barrier, inc=1, device_id=(me_y, peer(e)), device_id_type=MESH
        )
    for d, t in others:
        pl.semaphore_signal(
            barrier, inc=1, device_id=(at(d, t), me_z), device_id_type=MESH
        )

    half = chans // 2
    grids = []
    for x in range(planes):
        one = pltpu.make_async_copy(a_tab.at[me_z, x], a_v.at[x], a_sem.at[x])
        two = pltpu.make_async_copy(
            field.at[0:half, x], f_v.at[0:half, x], grid_sem.at[x]
        )
        one.start()
        two.start()
        grids.append((one, two))
    loads = [
        pltpu.make_async_copy(field.at[half:chans], f_v.at[half:chans], load_sem.at[0]),
        pltpu.make_async_copy(point, p_v, load_sem.at[1]),
        pltpu.make_async_copy(bias, bias_s, load_sem.at[2]),
        pltpu.make_async_copy(weight, w_v, load_sem.at[3]),
        pltpu.make_async_copy(ay_tab.at[block], ay_v, load_sem.at[4]),
        pltpu.make_async_copy(sy_tab.at[block], sy_v, load_sem.at[5]),
        pltpu.make_async_copy(b_tab.at[me_z], b_out, load_sem.at[6]),
    ]
    for load in loads:
        load.start()

    e1[...] = select(
        e1.shape, lambda r: r >> bits(rows), lambda c: c >> bits(chans)
    ).astype(BF16)
    e2[...] = select(
        e2.shape, lambda r: r & (chans - 1), lambda c: c >> bits(rows)
    ).astype(BF16)
    spread[...] = select(spread.shape, lambda r: r >> bits(rows), lambda c: c).astype(BF16)

    pair_order = range(pairs - 1, -1, -1)
    started = []
    first = {}
    for h in range(2):
        if h == 1:
            loads[0].wait()
        total = jnp.zeros((planes * KZ, HALF), F32)
        for x in range(planes):
            if h == 0:
                for load in grids[x]:
                    load.wait()
            grid = f_v[h * half:(h + 1) * half, x].reshape(HALF, depth)
            total += lax.dot_general(
                a_v[x], grid, (((1,), (1,)), ((), ())), preferred_element_type=F32
            )
        part[h] = total.reshape(n_z * pairs, 2 * SHARE, HALF).astype(BF16)
        if h == 0:
            pl.semaphore_wait(barrier, n_z - 1 + len(others))
        for p in pair_order:
            ip = lax.div(flip(mine, 2 * p), 2)
            for e in range(1, n_z):
                copy = pltpu.make_async_remote_copy(
                    src_ref=part.at[h, peer(e) * pairs + ip],
                    dst_ref=got1.at[e - 1, h, ip],
                    send_sem=send1.at[e - 1, h, p],
                    recv_sem=recv1.at[e - 1, h, p],
                    device_id=(me_y, peer(e)),
                    device_id_type=MESH,
                )
                copy.start()
                first[e, h, p] = copy
                started.append(copy)

    loads[1].wait()
    wide = lax.dot_general(
        spread[...], p_v[...], (((1,), (1,)), ((), ())), preferred_element_type=F32
    ).astype(BF16)
    wide = lax.dot_general(
        wide, spread[...], (((1,), (1,)), ((), ())), preferred_element_type=F32
    )
    same = select(wide.shape, lambda r: r & (rows - 1), lambda c: c & (rows - 1))
    kron[...] = (wide * same).astype(BF16)
    loads[2].wait()
    for o in range(chans):
        bias_v[o * rows:(o + 1) * rows, :] = jnp.full((rows, depth), bias_s[o], F32)

    def pointwise(x):
        grid = f_v[:, x].reshape(chans * rows, depth)
        value = jnp.dot(kron[...], grid, preferred_element_type=F32)
        local[x] = value + bias_v[...]

    pointwise(0)

    second = {}
    for p in pair_order:
        ip = lax.div(flip(mine, 2 * p), 2)
        sums = []
        for h in range(2):
            total = part[h, me_z * pairs + ip].astype(F32)
            for e in range(1, n_z):
                first[e, h, p].wait_recv()
                total += got1[e - 1, h, ip].astype(F32)
            sums.append(total)
        for odd in range(2):
            side = slice(odd * SHARE, (odd + 1) * SHARE)
            owned[ip * 2 + odd] = jnp.concatenate(
                [sums[0][side], sums[1][side]], axis=0
            ).astype(BF16)
        for d in (2 * p + 1, 2 * p):
            for t in range(group):
                if d == 0 and t == 0:
                    continue
                copy = pltpu.make_async_remote_copy(
                    src_ref=owned.at[flip(mine, d)],
                    dst_ref=got2.at[me_y],
                    send_sem=send2.at[d * group + t],
                    recv_sem=recv2.at[d * group + t],
                    device_id=(at(d, t), me_z),
                    device_id_type=MESH,
                )
                copy.start()
                second[d, t] = copy
                started.append(copy)
    got2[me_y] = owned[mine]

    for x in range(1, 4):
        pointwise(x)

    for load in loads[3:6]:
        load.wait()
    for d, t in others:
        second[d, t].wait_recv()
    for h in range(2):
        pieces = [got2[s].astype(F32)[h * SHARE:(h + 1) * SHARE] for s in range(n_y)]
        for j in range(first_share):
            total = pieces[0] * ay_v[j, 0:1, :]
            for s in range(1, n_y):
                total += pieces[s] * ay_v[j, s:s + 1, :]
            u_v[j, :, h * HALF:(h + 1) * HALF] = total

    mode_rows = first_share * SHARE
    spectrum = jnp.dot(
        u_v[...].reshape(mode_rows, 2 * HALF).astype(BF16), e1[...], preferred_element_type=F32
    )
    terms = spectrum * w_v[...].astype(F32).reshape(mode_rows, chans * chans)
    mixed = jnp.dot(terms.astype(BF16), e2[...], preferred_element_type=F32)
    m_v[...] = mixed.reshape(first_share, SHARE, 2 * HALF)

    third = {}
    for d, t in others[::-1] + [(0, 0)]:
        target = at(d, t)
        synth = sy_v[target]
        sides = []
        for h in range(2):
            total = m_v[0, :, h * HALF:(h + 1) * HALF] * synth[0:1, :]
            for j in range(1, first_share):
                total += m_v[j, :, h * HALF:(h + 1) * HALF] * synth[j:j + 1, :]
            sides.append(total)
        value = jnp.concatenate(sides, axis=0).astype(BF16)
        if d == 0 and t == 0:
            got3[me_y] = value
            continue
        tout[target] = value
        copy = pltpu.make_async_remote_copy(
            src_ref=tout.at[target],
            dst_ref=got3.at[me_y],
            send_sem=send3.at[d * group + t],
            recv_sem=recv3.at[d * group + t],
            device_id=(target, me_z),
            device_id_type=MESH,
        )
        copy.start()
        third[d, t] = copy
        started.append(copy)

    fourth = []
    for d in [0, *range(planes - 1, 0, -1)]:
        total = None
        for t in range(group):
            if (d, t) != (0, 0):
                third[d, t].wait_recv()
            piece = got3[came(d, t)]
            if group > 1:
                piece = piece.astype(F32)
            total = piece if total is None else total + piece
        slot = me_z * planes + flip(mine, d)
        modes[slot] = total.astype(BF16)
        for e in range(1, n_z):
            copy = pltpu.make_async_remote_copy(
                src_ref=modes.at[slot],
                dst_ref=modes.at[slot],
                send_sem=send4.at[e - 1, d],
                recv_sem=recv4.at[e - 1, d],
                device_id=(me_y, peer(e)),
                device_id_type=MESH,
            )
            copy.start()
            fourth.append(copy)

    for x in range(4, planes):
        pointwise(x)
    loads[6].wait()

    for copy in fourth:
        copy.wait_recv()
    for h in range(2):
        value = modes[...].astype(F32)[:, h * SHARE:(h + 1) * SHARE, :]
        value = value.reshape(planes * KZ, HALF)
        gt_out[h * HALF:(h + 1) * HALF, :] = value.T.astype(BF16)
    for copy in started + fourth:
        copy.wait_send()


def grid_kernel(local, gt, synth, out, o_v, out_sem):
    planes, _, depth = local.shape
    chans, _, rows, _ = o_v.shape
    stores = []
    scale = math.sqrt(2.0 / math.pi)
    for x in range(planes):
        value = local[x] + jnp.dot(gt[...], synth[x], preferred_element_type=F32)
        inner = value * (scale + (scale * 0.044715) * (value * value))
        small = 0.5 * value
        value = small + small * jnp.tanh(inner)
        o_v[:, x] = value.astype(BF16).reshape(chans, rows, depth)
        store = pltpu.make_async_copy(o_v.at[:, x], out.at[:, x], out_sem.at[x])
        store.start()
        stores.append(store)
    for store in stores:
        store.wait()


def shards(n_y, n_z, field, spectral_weight, point_weight, bias):
    chans, planes, rows, depth = field.shape
    first_share, depth_share = spectral_weight.shape[:2]
    assert depth_share == SHARE and chans * rows == 2 * HALF and first_share <= KY
    assert n_y % planes == 0 and depth_share * n_z == KZ and planes % 2 == 0
    a_tab, b_tab, ay_tab, sy_tab = tables(n_y, n_z, planes, rows, depth, first_share)
    pairs = planes // 2
    vmem = pl.BlockSpec(memory_space=pltpu.VMEM)
    hbm = pl.BlockSpec(memory_space=pltpu.HBM)
    wide = 2 * HALF
    dma = pltpu.SemaphoreType.DMA
    operands = [field, a_tab, b_tab, spectral_weight, point_weight, bias, ay_tab, sy_tab]
    local, gt, synth = pl.pallas_call(
        functools.partial(spectral_kernel, n_y, n_z),
        out_shape=(
            pltpu.VMEM((planes, wide, depth), F32),
            pltpu.VMEM((wide, planes * KZ), BF16),
            pltpu.VMEM(b_tab.shape[1:], BF16),
        ),
        in_specs=[hbm] * len(operands),
        out_specs=(vmem, vmem, vmem),
        scratch_shapes=[
            pltpu.VMEM(field.shape, BF16),
            pltpu.VMEM(a_tab.shape[1:], BF16),
            pltpu.VMEM(spectral_weight.shape, BF16),
            pltpu.VMEM(point_weight.shape, BF16),
            pltpu.SMEM(bias.shape, F32),
            pltpu.VMEM((wide, depth), F32),
            pltpu.VMEM(ay_tab.shape[1:], F32),
            pltpu.VMEM(sy_tab.shape[1:], F32),
            pltpu.VMEM((wide, chans * chans), BF16),
            pltpu.VMEM((chans * chans, wide), BF16),
            pltpu.VMEM((wide, chans), BF16),
            pltpu.VMEM((wide, wide), BF16),
            pltpu.VMEM((2, n_z * pairs, 2 * SHARE, HALF), BF16),
            pltpu.VMEM((n_z - 1, 2, pairs, 2 * SHARE, HALF), BF16),
            pltpu.VMEM((planes, 2 * SHARE, HALF), BF16),
            pltpu.VMEM((n_y, 2 * SHARE, HALF), BF16),
            pltpu.VMEM((first_share, SHARE, wide), F32),
            pltpu.VMEM((first_share, SHARE, wide), F32),
            pltpu.VMEM((n_y, 2 * SHARE, HALF), BF16),
            pltpu.VMEM((n_y, 2 * SHARE, HALF), BF16),
            pltpu.VMEM((n_z * planes, 2 * SHARE, HALF), BF16),
            dma((7,)),
            dma((planes,)),
            dma((planes,)),
            dma((n_z - 1, 2, pairs)),
            dma((n_z - 1, 2, pairs)),
            dma((n_y,)),
            dma((n_y,)),
            dma((n_y,)),
            dma((n_y,)),
            dma((n_z - 1, planes)),
            dma((n_z - 1, planes)),
        ],
        compiler_params=pltpu.CompilerParams(
            collective_id=0, has_side_effects=True, vmem_limit_bytes=40 * 1024 * 1024
        ),
        name="spectral",
    )(*(pltpu.with_memory_space_constraint(value, pltpu.HBM) for value in operands))
    return pl.pallas_call(
        grid_kernel,
        out_shape=jax.ShapeDtypeStruct(field.shape, BF16),
        in_specs=[vmem] * 3,
        out_specs=hbm,
        scratch_shapes=[pltpu.VMEM(field.shape, BF16), dma((planes,))],
        compiler_params=pltpu.CompilerParams(vmem_limit_bytes=40 * 1024 * 1024),
        name="grid",
    )(local, gt, synth)


def solution(mesh):
    return jax.shard_map(
        functools.partial(shards, mesh.shape["gy"], mesh.shape["gz"]),
        mesh=mesh,
        in_specs=(P(None, None, "gy", "gz"), P("gy", "gz", None), P(), P()),
        out_specs=P(None, None, "gy", "gz"),
        check_vma=False,
    )
```

```python
import functools
import math

import jax
import jax.numpy as jnp
import ml_dtypes
import numpy as np
from jax import lax
from jax.experimental import pallas as pl
from jax.experimental.pallas import tpu as pltpu
from jax.sharding import PartitionSpec as P

KY = 32
KZ = 32
BF16 = jnp.bfloat16
F32 = jnp.float32
MESH = pl.DeviceIdType.MESH
SHARE = 8
HALF = 256


def basis(count, length, norm):
    modes = np.arange(count)[:, None]
    spots = np.arange(length)[None, :]
    value = norm * np.cos(np.pi * modes * (spots + 0.5) / length)
    return np.where(modes == 0, value * math.sqrt(0.5), value)


def tables(n_y, n_z, planes, rows, depth, first_share):
    total_rows, total_depth = rows * n_y, depth * n_z
    az = basis(KZ, total_depth, math.sqrt(2.0 / total_depth))
    az = az.astype(np.float32).astype(ml_dtypes.bfloat16).astype(np.float64)
    ax = basis(planes, planes, math.sqrt(2.0 / planes))
    sz = basis(KZ, total_depth, math.sqrt(2.0 / KZ))

    def joint(x_basis, z_basis):
        z = z_basis.reshape(n_z // 2, 2, SHARE, n_z, depth)
        both = np.einsum("ix,hlkdz->dxlhikz", x_basis, z)
        return both.reshape(n_z, planes, planes * KZ, depth).astype(ml_dtypes.bfloat16)

    ay = basis(KY, total_rows, math.sqrt(2.0 / total_rows))
    sy = basis(KY, total_rows, math.sqrt(2.0 / KY))
    blocks = KY // first_share

    def lanes(y_basis):
        parts = y_basis.reshape(blocks, first_share, n_y, rows)
        return np.tile(parts, (1, 1, 1, HALF // rows)).astype(np.float32)

    analysis_y = lanes(ay)
    synth_y = np.ascontiguousarray(np.swapaxes(lanes(sy), 1, 2))
    return joint(ax, az), joint(ax, sz), analysis_y, synth_y


def bits(count):
    assert count & (count - 1) == 0
    return count.bit_length() - 1


def select(shape, row_of, column_of):
    r = row_of(lax.broadcasted_iota(jnp.int32, shape, 0))
    c = column_of(lax.broadcasted_iota(jnp.int32, shape, 1))
    return jnp.where(r == c, 1.0, 0.0).astype(F32)


def spectral_kernel(
    n_y, n_z, field, a_tab, b_tab, weight, point, bias, ay_tab, sy_tab, local, gt_out, b_out,
    f_v, a_v, w_v, p_v, bias_s, bias_v, ay_v, sy_v, e1, e2, spread, kron,
    part, got1, owned, got2, u_v, m_v, tout, got3, modes,
    load_sem, grid_sem, a_sem, send1, recv1, send2, recv2, send3, recv3, send4, recv4,
):
    me_y, me_z = lax.axis_index("gy"), lax.axis_index("gz")
    chans, planes, rows, depth = f_v.shape
    pairs = planes // 2
    group = n_y // planes
    highs = n_z // 2
    high, low = lax.div(me_z, 2), lax.rem(me_z, 2)
    near = high * 2 + 1 - low
    first_share = w_v.shape[0]
    mine, place = lax.div(me_y, group), lax.rem(me_y, group)
    block = place if first_share < KY else 0
    others = [
        (d, t, u) for d in range(planes) for t in range(group) for u in range(highs)
    ][1:]

    def flip(index, mask):
        for k in range(bits(planes)):
            if mask >> k & 1:
                bit = lax.rem(lax.div(index, 1 << k), 2)
                index = index + (1 << k) * (1 - 2 * bit)
        return index

    def at(d, t):
        return flip(mine, d) * group + lax.rem(place + t, group)

    def came(d, t):
        return flip(mine, d) * group + lax.rem(place - t + group, group)

    def high_at(u):
        return lax.rem(high + u, highs)

    def arrived(blocks, semaphore):
        pltpu.make_async_copy(blocks, blocks, semaphore).wait()

    barrier = pltpu.get_barrier_semaphore()
    pl.semaphore_signal(barrier, inc=1, device_id=(me_y, near), device_id_type=MESH)
    for d, t, u in others:
        pl.semaphore_signal(
            barrier, inc=1, device_id=(at(d, t), high_at(u) * 2 + low), device_id_type=MESH
        )

    half = chans // 2
    grids = []
    for x in range(planes):
        one = pltpu.make_async_copy(a_tab.at[me_z, x], a_v.at[x], a_sem.at[x])
        two = pltpu.make_async_copy(
            field.at[0:half, x], f_v.at[0:half, x], grid_sem.at[x]
        )
        one.start()
        two.start()
        grids.append((one, two))
    loads = [
        pltpu.make_async_copy(field.at[half:chans], f_v.at[half:chans], load_sem.at[0]),
        pltpu.make_async_copy(point, p_v, load_sem.at[1]),
        pltpu.make_async_copy(bias, bias_s, load_sem.at[2]),
        pltpu.make_async_copy(weight, w_v, load_sem.at[3]),
        pltpu.make_async_copy(ay_tab.at[block], ay_v, load_sem.at[4]),
        pltpu.make_async_copy(sy_tab.at[block], sy_v, load_sem.at[5]),
        pltpu.make_async_copy(b_tab.at[me_z], b_out, load_sem.at[6]),
    ]
    for load in loads:
        load.start()

    e1[...] = select(
        e1.shape, lambda r: r >> bits(rows), lambda c: c >> bits(chans)
    ).astype(BF16)

    pair_order = range(pairs - 1, -1, -1)
    for h in range(2):
        if h == 1:
            loads[0].wait()
        total = jnp.zeros((planes * KZ, HALF), F32)
        for x in range(planes):
            if h == 0:
                for load in grids[x]:
                    load.wait()
            grid = f_v[h * half:(h + 1) * half, x].reshape(HALF, depth)
            total += lax.dot_general(
                a_v[x], grid, (((1,), (1,)), ((), ())), preferred_element_type=F32
            )
        part[h] = total.reshape(2, highs * pairs, 2 * SHARE, HALF).astype(BF16)
        if h == 0:
            pl.semaphore_wait(barrier, 1 + len(others))
        pltpu.make_async_remote_copy(
            src_ref=part.at[h, 1 - low],
            dst_ref=got1.at[h],
            send_sem=send1,
            recv_sem=recv1.at[h],
            device_id=(me_y, near),
            device_id_type=MESH,
        ).start()

    e2[...] = select(
        e2.shape, lambda r: r & (chans - 1), lambda c: c >> bits(rows)
    ).astype(BF16)
    for h in range(2):
        arrived(got1.at[h], recv1.at[h])
    for p in pair_order:
        ip = lax.div(flip(mine, 2 * p), 2)
        for u in range(highs):
            slot = high_at(u) * pairs + ip
            sums = []
            for h in range(2):
                sums.append(part[h, low, slot].astype(F32) + got1[h, slot].astype(F32))
            for odd in range(2):
                side = slice(odd * SHARE, (odd + 1) * SHARE)
                owned[high_at(u) * planes + ip * 2 + odd] = jnp.concatenate(
                    [sums[0][side], sums[1][side]], axis=0
                ).astype(BF16)
        for d in (2 * p + 1, 2 * p):
            for t in range(group):
                for u in range(highs):
                    if d == 0 and t == 0 and u == 0:
                        continue
                    pltpu.make_async_remote_copy(
                        src_ref=owned.at[high_at(u) * planes + flip(mine, d)],
                        dst_ref=got2.at[high * n_y + me_y],
                        send_sem=send2,
                        recv_sem=recv2,
                        device_id=(at(d, t), high_at(u) * 2 + low),
                        device_id_type=MESH,
                    ).start()
    got2[high * n_y + me_y] = owned[high * planes + mine]

    spread[...] = select(spread.shape, lambda r: r >> bits(rows), lambda c: c).astype(BF16)

    loads[1].wait()
    wide = lax.dot_general(
        spread[...], p_v[...], (((1,), (1,)), ((), ())), preferred_element_type=F32
    ).astype(BF16)
    wide = lax.dot_general(
        wide, spread[...], (((1,), (1,)), ((), ())), preferred_element_type=F32
    )
    same = select(wide.shape, lambda r: r & (rows - 1), lambda c: c & (rows - 1))
    kron[...] = (wide * same).astype(BF16)
    loads[2].wait()
    for o in range(chans):
        bias_v[o * rows:(o + 1) * rows, :] = jnp.full((rows, depth), bias_s[o], F32)

    def pointwise(x):
        grid = f_v[:, x].reshape(chans * rows, depth)
        value = jnp.dot(kron[...], grid, preferred_element_type=F32)
        local[x] = value + bias_v[...]

    for x in range(4):
        pointwise(x)

    for load in loads[3:6]:
        load.wait()
    arrived(got2.at[0:len(others)], recv2)
    for h in range(2):
        pieces = []
        for s in range(n_y):
            total = got2[s].astype(F32)
            for u in range(1, highs):
                total += got2[u * n_y + s].astype(F32)
            pieces.append(total[h * SHARE:(h + 1) * SHARE])
        for j in range(first_share):
            total = pieces[0] * ay_v[j, 0:1, :]
            for s in range(1, n_y):
                total += pieces[s] * ay_v[j, s:s + 1, :]
            u_v[j, :, h * HALF:(h + 1) * HALF] = total

    mode_rows = first_share * SHARE
    spectrum = jnp.dot(
        u_v[...].reshape(mode_rows, 2 * HALF).astype(BF16), e1[...], preferred_element_type=F32
    )
    terms = spectrum * w_v[...].astype(F32).reshape(mode_rows, chans * chans)
    mixed = jnp.dot(terms.astype(BF16), e2[...], preferred_element_type=F32)
    m_v[...] = mixed.reshape(first_share, SHARE, 2 * HALF)

    sets = [range(1 << k, 2 << k) for k in range(bits(planes) - 1, 0, -1)] + [range(2)]
    landing = modes if group == 1 else got3

    def land(index, sender):
        start = low * highs * planes if group == 1 else 0
        return start + index * n_y + sender

    for c, members in enumerate(sets):
        for d in members[::-1]:
            for t in range(group - 1, -1, -1):
                target = at(d, t)
                sides = []
                for h in range(2):
                    total = m_v[0, :, h * HALF:(h + 1) * HALF] * sy_v[target, 0:1, :]
                    for j in range(1, first_share):
                        total += m_v[j, :, h * HALF:(h + 1) * HALF] * sy_v[target, j:j + 1, :]
                    sides.append(total)
                tout[target] = jnp.concatenate(sides, axis=0).astype(BF16)
                for u in range(highs):
                    if d == 0 and t == 0 and u == 0:
                        landing[land(high, me_y)] = tout[target]
                        continue
                    pltpu.make_async_remote_copy(
                        src_ref=tout.at[target],
                        dst_ref=landing.at[land(high, me_y)],
                        send_sem=send3,
                        recv_sem=recv3.at[c],
                        device_id=(target, high_at(u) * 2 + low),
                        device_id_type=MESH,
                    ).start()

    for x in range(4, planes):
        pointwise(x)
    loads[6].wait()

    for c, members in enumerate(sets):
        count = len(members) * group * highs - (1 if 0 in members else 0)
        arrived(landing.at[0:count], recv3.at[c])
        size = len(members)
        first = lax.div(flip(mine, members[0]), size) * size
        for index in range(highs):
            start = (low * highs + index) * planes
            if group > 1:
                for d in members:
                    total = landing[land(index, came(d, 0))].astype(F32)
                    for t in range(1, group):
                        total += landing[land(index, came(d, t))].astype(F32)
                    modes[start + flip(mine, d)] = total.astype(BF16)
            pltpu.make_async_remote_copy(
                src_ref=modes.at[pl.ds(start + first, size)],
                dst_ref=modes.at[pl.ds(start + first, size)],
                send_sem=send4,
                recv_sem=recv4,
                device_id=(me_y, near),
                device_id_type=MESH,
            ).start()

    arrived(modes.at[0:highs * planes], recv4)
    for h in range(2):
        value = modes[...].astype(F32)[:, h * SHARE:(h + 1) * SHARE, :]
        value = value.reshape(planes * KZ, HALF)
        gt_out[h * HALF:(h + 1) * HALF, :] = value.T.astype(BF16)
    arrived(got1, send1)
    arrived(got2.at[0:len(others)], send2)
    arrived(got2.at[0:len(others)], send3)
    arrived(modes.at[0:highs * planes], send4)


def grid_kernel(local, gt, synth, out, o_v, out_sem):
    planes, _, depth = local.shape
    chans, _, rows, _ = o_v.shape
    stores = []
    scale = math.sqrt(2.0 / math.pi)
    for x in range(planes):
        value = local[x] + jnp.dot(gt[...], synth[x], preferred_element_type=F32)
        inner = value * (scale + (scale * 0.044715) * (value * value))
        small = 0.5 * value
        value = small + small * jnp.tanh(inner)
        o_v[:, x] = value.astype(BF16).reshape(chans, rows, depth)
        store = pltpu.make_async_copy(o_v.at[:, x], out.at[:, x], out_sem.at[x])
        store.start()
        stores.append(store)
    for store in stores:
        store.wait()


def shards(n_y, n_z, field, spectral_weight, point_weight, bias):
    chans, planes, rows, depth = field.shape
    first_share, depth_share = spectral_weight.shape[:2]
    assert depth_share == SHARE and chans * rows == 2 * HALF and first_share <= KY
    assert n_y % planes == 0 and depth_share * n_z == KZ and planes % 2 == 0 and n_z % 2 == 0
    a_tab, b_tab, ay_tab, sy_tab = tables(n_y, n_z, planes, rows, depth, first_share)
    pairs, highs = planes // 2, n_z // 2
    vmem = pl.BlockSpec(memory_space=pltpu.VMEM)
    hbm = pl.BlockSpec(memory_space=pltpu.HBM)
    wide = 2 * HALF
    dma = pltpu.SemaphoreType.DMA
    operands = [field, a_tab, b_tab, spectral_weight, point_weight, bias, ay_tab, sy_tab]
    local, gt, synth = pl.pallas_call(
        functools.partial(spectral_kernel, n_y, n_z),
        out_shape=(
            pltpu.VMEM((planes, wide, depth), F32),
            pltpu.VMEM((wide, planes * KZ), BF16),
            pltpu.VMEM(b_tab.shape[1:], BF16),
        ),
        in_specs=[hbm] * len(operands),
        out_specs=(vmem, vmem, vmem),
        scratch_shapes=[
            pltpu.VMEM(field.shape, BF16),
            pltpu.VMEM(a_tab.shape[1:], BF16),
            pltpu.VMEM(spectral_weight.shape, BF16),
            pltpu.VMEM(point_weight.shape, BF16),
            pltpu.SMEM(bias.shape, F32),
            pltpu.VMEM((wide, depth), F32),
            pltpu.VMEM(ay_tab.shape[1:], F32),
            pltpu.VMEM(sy_tab.shape[1:], F32),
            pltpu.VMEM((wide, chans * chans), BF16),
            pltpu.VMEM((chans * chans, wide), BF16),
            pltpu.VMEM((wide, chans), BF16),
            pltpu.VMEM((wide, wide), BF16),
            pltpu.VMEM((2, 2, highs * pairs, 2 * SHARE, HALF), BF16),
            pltpu.VMEM((2, highs * pairs, 2 * SHARE, HALF), BF16),
            pltpu.VMEM((highs * planes, 2 * SHARE, HALF), BF16),
            pltpu.VMEM((highs * n_y, 2 * SHARE, HALF), BF16),
            pltpu.VMEM((first_share, SHARE, wide), F32),
            pltpu.VMEM((first_share, SHARE, wide), F32),
            pltpu.VMEM((n_y, 2 * SHARE, HALF), BF16),
            pltpu.VMEM((highs * n_y, 2 * SHARE, HALF), BF16),
            pltpu.VMEM((n_z * planes, 2 * SHARE, HALF), BF16),
            dma((7,)),
            dma((planes,)),
            dma((planes,)),
            dma(()),
            dma((2,)),
            dma(()),
            dma(()),
            dma(()),
            dma((bits(planes),)),
            dma(()),
            dma(()),
        ],
        compiler_params=pltpu.CompilerParams(
            collective_id=0, has_side_effects=True, vmem_limit_bytes=40 * 1024 * 1024
        ),
        name="spectral",
    )(*(pltpu.with_memory_space_constraint(value, pltpu.HBM) for value in operands))
    return pl.pallas_call(
        grid_kernel,
        out_shape=jax.ShapeDtypeStruct(field.shape, BF16),
        in_specs=[vmem] * 3,
        out_specs=hbm,
        scratch_shapes=[pltpu.VMEM(field.shape, BF16), dma((planes,))],
        compiler_params=pltpu.CompilerParams(vmem_limit_bytes=40 * 1024 * 1024),
        name="grid",
    )(local, gt, synth)


def solution(mesh):
    return jax.shard_map(
        functools.partial(shards, mesh.shape["gy"], mesh.shape["gz"]),
        mesh=mesh,
        in_specs=(P(None, None, "gy", "gz"), P("gy", "gz", None), P(), P()),
        out_specs=P(None, None, "gy", "gz"),
        check_vma=False,
    )
```

```python
import functools
import math

import jax
import jax.numpy as jnp
import ml_dtypes
import numpy as np
from jax import lax
from jax.experimental import pallas as pl
from jax.experimental.pallas import tpu as pltpu
from jax.sharding import PartitionSpec as P

KY = 32
KZ = 32
BF16 = jnp.bfloat16
F32 = jnp.float32
MESH = pl.DeviceIdType.MESH
SHARE = 8
HALF = 256


def basis(count, length, norm):
    modes = np.arange(count)[:, None]
    spots = np.arange(length)[None, :]
    value = norm * np.cos(np.pi * modes * (spots + 0.5) / length)
    return np.where(modes == 0, value * math.sqrt(0.5), value)


def tables(n_y, n_z, planes, rows, depth, first_share):
    total_rows, total_depth = rows * n_y, depth * n_z
    az = basis(KZ, total_depth, math.sqrt(2.0 / total_depth))
    az = az.astype(np.float32).astype(ml_dtypes.bfloat16).astype(np.float64)
    ax = basis(planes, planes, math.sqrt(2.0 / planes))
    sz = basis(KZ, total_depth, math.sqrt(2.0 / KZ))

    def joint(x_basis, z_basis):
        z = z_basis.reshape(n_z // 2, 2, SHARE, n_z, depth)
        both = np.einsum("ix,hlkdz->dxlhikz", x_basis, z)
        return both.reshape(n_z, planes, planes * KZ, depth).astype(ml_dtypes.bfloat16)

    ay = basis(KY, total_rows, math.sqrt(2.0 / total_rows))
    sy = basis(KY, total_rows, math.sqrt(2.0 / KY))
    blocks = KY // first_share

    def lanes(y_basis):
        parts = y_basis.reshape(blocks, first_share, n_y, rows)
        return np.tile(parts, (1, 1, 1, HALF // rows)).astype(np.float32)

    analysis_y = lanes(ay)
    synth_y = np.ascontiguousarray(np.swapaxes(lanes(0.5 * sy), 1, 2))
    synth = joint(ax, sz).reshape(n_z, planes, 2, planes * KZ // 2, depth)
    return joint(ax, az), synth, analysis_y, synth_y


def bits(count):
    assert count & (count - 1) == 0
    return count.bit_length() - 1


def select(shape, row_of, column_of):
    r = row_of(lax.broadcasted_iota(jnp.int32, shape, 0))
    c = column_of(lax.broadcasted_iota(jnp.int32, shape, 1))
    return jnp.where(r == c, 1.0, 0.0).astype(F32)


def spectral_kernel(
    n_y, n_z, field, a_tab, b_tab, weight, point, bias, ay_tab, sy_tab, local, gt_out, b_out,
    f_v, a_v, w_v, p_v, bias_s, bias_v, ay_v, sy_v, e1, e2, spread, kron,
    part, got1, owned, got2, u_v, m_v, tout, got3, modes,
    load_sem, grid_sem, a_sem, send1, recv1, send2, recv2, send3, recv3, send4, recv4,
):
    me_y, me_z = lax.axis_index("gy"), lax.axis_index("gz")
    chans, planes, rows, depth = f_v.shape
    pairs = planes // 2
    group = n_y // planes
    highs = n_z // 2
    high, low = lax.div(me_z, 2), lax.rem(me_z, 2)
    near = high * 2 + 1 - low
    first_share = w_v.shape[0]
    mine, place = lax.div(me_y, group), lax.rem(me_y, group)
    block = place if first_share < KY else 0
    others = [
        (d, t, u) for d in range(planes) for t in range(group) for u in range(highs)
    ][1:]

    def flip(index, mask):
        for k in range(bits(planes)):
            if mask >> k & 1:
                bit = lax.rem(lax.div(index, 1 << k), 2)
                index = index + (1 << k) * (1 - 2 * bit)
        return index

    def at(d, t):
        return flip(mine, d) * group + lax.rem(place + t, group)

    def came(d, t):
        return flip(mine, d) * group + lax.rem(place - t + group, group)

    def high_at(u):
        return lax.rem(high + u, highs)

    def arrived(blocks, semaphore):
        pltpu.make_async_copy(blocks, blocks, semaphore).wait()

    barrier = pltpu.get_barrier_semaphore()
    pl.semaphore_signal(barrier, inc=1, device_id=(me_y, near), device_id_type=MESH)
    for d, t, u in others:
        pl.semaphore_signal(
            barrier, inc=1, device_id=(at(d, t), high_at(u) * 2 + low), device_id_type=MESH
        )

    half = chans // 2
    side = planes * KZ // 2
    grids = []
    for x in range(planes):
        one = pltpu.make_async_copy(a_tab.at[me_z, x], a_v.at[x], a_sem.at[x])
        two = pltpu.make_async_copy(
            field.at[0:half, x], f_v.at[0:half, x], grid_sem.at[x]
        )
        one.start()
        two.start()
        grids.append((one, two))
    loads = [
        pltpu.make_async_copy(field.at[half:chans], f_v.at[half:chans], load_sem.at[0]),
        pltpu.make_async_copy(point, p_v, load_sem.at[1]),
        pltpu.make_async_copy(bias, bias_s, load_sem.at[2]),
        pltpu.make_async_copy(weight, w_v, load_sem.at[3]),
        pltpu.make_async_copy(ay_tab.at[block], ay_v, load_sem.at[4]),
        pltpu.make_async_copy(sy_tab.at[block], sy_v, load_sem.at[5]),
        pltpu.make_async_copy(b_tab.at[me_z, :, low], b_out.at[:, 0:side], load_sem.at[6]),
        pltpu.make_async_copy(
            b_tab.at[me_z, :, 1 - low], b_out.at[:, side:2 * side], load_sem.at[7]
        ),
    ]
    for load in loads:
        load.start()

    e1[...] = select(
        e1.shape, lambda r: r >> bits(rows), lambda c: c >> bits(chans)
    ).astype(BF16)

    pair_order = range(pairs - 1, -1, -1)
    for h in range(2):
        if h == 1:
            loads[0].wait()
        total = jnp.zeros((planes * KZ, HALF), F32)
        for x in range(planes):
            if h == 0:
                for load in grids[x]:
                    load.wait()
            grid = f_v[h * half:(h + 1) * half, x].reshape(HALF, depth)
            total += lax.dot_general(
                a_v[x], grid, (((1,), (1,)), ((), ())), preferred_element_type=F32
            )
        part[h] = total.reshape(2, highs * pairs, 2 * SHARE, HALF).astype(BF16)
        if h == 0:
            pl.semaphore_wait(barrier, 1 + len(others))
        pltpu.make_async_remote_copy(
            src_ref=part.at[h, 1 - low],
            dst_ref=got1.at[h],
            send_sem=send1,
            recv_sem=recv1.at[h],
            device_id=(me_y, near),
            device_id_type=MESH,
        ).start()

    e2[...] = select(
        e2.shape, lambda r: r & (chans - 1), lambda c: c >> bits(rows)
    ).astype(BF16)
    for h in range(2):
        arrived(got1.at[h], recv1.at[h])
    for p in pair_order:
        ip = lax.div(flip(mine, 2 * p), 2)
        for u in range(highs):
            slot = high_at(u) * pairs + ip
            sums = []
            for h in range(2):
                sums.append(part[h, low, slot].astype(F32) + got1[h, slot].astype(F32))
            for odd in range(2):
                of = slice(odd * SHARE, (odd + 1) * SHARE)
                owned[high_at(u) * planes + ip * 2 + odd] = jnp.concatenate(
                    [sums[0][of], sums[1][of]], axis=0
                ).astype(BF16)
        for d in (2 * p + 1, 2 * p):
            for t in range(group):
                for u in range(highs):
                    if d == 0 and t == 0 and u == 0:
                        continue
                    pltpu.make_async_remote_copy(
                        src_ref=owned.at[high_at(u) * planes + flip(mine, d)],
                        dst_ref=got2.at[high * n_y + me_y],
                        send_sem=send2,
                        recv_sem=recv2,
                        device_id=(at(d, t), high_at(u) * 2 + low),
                        device_id_type=MESH,
                    ).start()
    got2[high * n_y + me_y] = owned[high * planes + mine]

    spread[...] = select(spread.shape, lambda r: r >> bits(rows), lambda c: c).astype(BF16)

    loads[1].wait()
    wide = lax.dot_general(
        spread[...], p_v[...], (((1,), (1,)), ((), ())), preferred_element_type=F32
    ).astype(BF16)
    wide = lax.dot_general(
        wide, spread[...], (((1,), (1,)), ((), ())), preferred_element_type=F32
    )
    same = select(wide.shape, lambda r: r & (rows - 1), lambda c: c & (rows - 1))
    kron[...] = (wide * (0.5 * same)).astype(BF16)
    loads[2].wait()
    for o in range(chans):
        bias_v[o * rows:(o + 1) * rows, :] = jnp.full((rows, depth), 0.5 * bias_s[o], F32)

    def pointwise(x):
        grid = f_v[:, x].reshape(chans * rows, depth)
        value = jnp.dot(kron[...], grid, preferred_element_type=F32)
        local[x] = value + bias_v[...]

    for x in range(4):
        pointwise(x)

    for load in loads[3:6]:
        load.wait()
    arrived(got2.at[0:len(others)], recv2)
    for h in range(2):
        pieces = []
        for s in range(n_y):
            total = got2[s].astype(F32)
            for u in range(1, highs):
                total += got2[u * n_y + s].astype(F32)
            pieces.append(total[h * SHARE:(h + 1) * SHARE])
        for j in range(first_share):
            total = pieces[0] * ay_v[j, 0:1, :]
            for s in range(1, n_y):
                total += pieces[s] * ay_v[j, s:s + 1, :]
            u_v[j, :, h * HALF:(h + 1) * HALF] = total

    mode_rows = first_share * SHARE
    spectrum = jnp.dot(
        u_v[...].reshape(mode_rows, 2 * HALF).astype(BF16), e1[...], preferred_element_type=F32
    )
    terms = spectrum * w_v[...].astype(F32).reshape(mode_rows, chans * chans)
    mixed = jnp.dot(terms.astype(BF16), e2[...], preferred_element_type=F32)
    m_v[...] = mixed.reshape(first_share, SHARE, 2 * HALF)

    sets = [range(1 << k, 2 << k) for k in range(bits(planes) - 1, 0, -1)] + [range(2)]
    landing = modes if group == 1 else got3

    def land(index, sender):
        start = low * highs * planes if group == 1 else 0
        return start + index * n_y + sender

    for c, members in enumerate(sets):
        places = [(d, t) for d in members[::-1] for t in range(group - 1, -1, -1)]
        for index in range(0, len(places), 4):
            batch = places[index:index + 4]
            sums = [[None, None] for _ in batch]
            for j in range(first_share):
                for h in range(2):
                    mode = m_v[j, :, h * HALF:(h + 1) * HALF]
                    for b, (d, t) in enumerate(batch):
                        term = mode * sy_v[at(d, t), j:j + 1, :]
                        sums[b][h] = term if j == 0 else sums[b][h] + term
            for b, (d, t) in enumerate(batch):
                target = at(d, t)
                tout[target] = jnp.concatenate(sums[b], axis=0).astype(BF16)
                for u in range(highs):
                    if d == 0 and t == 0 and u == 0:
                        landing[land(high, me_y)] = tout[target]
                        continue
                    pltpu.make_async_remote_copy(
                        src_ref=tout.at[target],
                        dst_ref=landing.at[land(high, me_y)],
                        send_sem=send3,
                        recv_sem=recv3.at[c],
                        device_id=(target, high_at(u) * 2 + low),
                        device_id_type=MESH,
                    ).start()

    for x in range(4, planes):
        pointwise(x)
    for load in loads[6:]:
        load.wait()

    for c, members in enumerate(sets):
        count = len(members) * group * highs - (1 if 0 in members else 0)
        arrived(landing.at[0:count], recv3.at[c])
        size = len(members)
        first = lax.div(flip(mine, members[0]), size) * size
        for index in range(highs):
            start = (low * highs + index) * planes
            if group > 1:
                for d in members:
                    total = landing[land(index, came(d, 0))].astype(F32)
                    for t in range(1, group):
                        total += landing[land(index, came(d, t))].astype(F32)
                    modes[start + flip(mine, d)] = total.astype(BF16)
            pltpu.make_async_remote_copy(
                src_ref=modes.at[pl.ds(start + first, size)],
                dst_ref=modes.at[pl.ds(start + first, size)],
                send_sem=send4,
                recv_sem=recv4,
                device_id=(me_y, near),
                device_id_type=MESH,
            ).start()

    def turn(part_of, start):
        value = modes[pl.ds(start, highs * planes)].astype(F32)
        for h in range(2):
            one = value[:, h * SHARE:(h + 1) * SHARE, :].reshape(side, HALF)
            gt_out[h * HALF:(h + 1) * HALF, part_of * side:(part_of + 1) * side] = one.T.astype(BF16)

    turn(0, low * highs * planes)
    arrived(modes.at[0:highs * planes], recv4)
    turn(1, (1 - low) * highs * planes)
    arrived(got1, send1)
    arrived(got2.at[0:len(others)], send2)
    arrived(got2.at[0:len(others)], send3)
    arrived(modes.at[0:highs * planes], send4)


def grid_kernel(local, gt, synth, out, o_v, out_sem):
    planes, _, depth = local.shape
    chans, _, rows, _ = o_v.shape
    stores = []
    scale = math.sqrt(2.0 / math.pi)
    for x in range(planes):
        value = local[x] + jnp.dot(gt[...], synth[x], preferred_element_type=F32)
        inner = value * (2.0 * scale + (8.0 * scale * 0.044715) * (value * value))
        value += value * jnp.tanh(inner)
        o_v[:, x] = value.astype(BF16).reshape(chans, rows, depth)
        store = pltpu.make_async_copy(o_v.at[:, x], out.at[:, x], out_sem.at[x])
        store.start()
        stores.append(store)
    for store in stores:
        store.wait()


def shards(n_y, n_z, field, spectral_weight, point_weight, bias):
    chans, planes, rows, depth = field.shape
    first_share, depth_share = spectral_weight.shape[:2]
    assert depth_share == SHARE and chans * rows == 2 * HALF and first_share <= KY
    assert n_y % planes == 0 and depth_share * n_z == KZ and planes % 2 == 0 and n_z % 2 == 0
    a_tab, b_tab, ay_tab, sy_tab = tables(n_y, n_z, planes, rows, depth, first_share)
    pairs, highs = planes // 2, n_z // 2
    vmem = pl.BlockSpec(memory_space=pltpu.VMEM)
    hbm = pl.BlockSpec(memory_space=pltpu.HBM)
    wide = 2 * HALF
    dma = pltpu.SemaphoreType.DMA
    operands = [field, a_tab, b_tab, spectral_weight, point_weight, bias, ay_tab, sy_tab]
    local, gt, synth = pl.pallas_call(
        functools.partial(spectral_kernel, n_y, n_z),
        out_shape=(
            pltpu.VMEM((planes, wide, depth), F32),
            pltpu.VMEM((wide, planes * KZ), BF16),
            pltpu.VMEM((planes, planes * KZ, depth), BF16),
        ),
        in_specs=[hbm] * len(operands),
        out_specs=(vmem, vmem, vmem),
        scratch_shapes=[
            pltpu.VMEM(field.shape, BF16),
            pltpu.VMEM(a_tab.shape[1:], BF16),
            pltpu.VMEM(spectral_weight.shape, BF16),
            pltpu.VMEM(point_weight.shape, BF16),
            pltpu.SMEM(bias.shape, F32),
            pltpu.VMEM((wide, depth), F32),
            pltpu.VMEM(ay_tab.shape[1:], F32),
            pltpu.VMEM(sy_tab.shape[1:], F32),
            pltpu.VMEM((wide, chans * chans), BF16),
            pltpu.VMEM((chans * chans, wide), BF16),
            pltpu.VMEM((wide, chans), BF16),
            pltpu.VMEM((wide, wide), BF16),
            pltpu.VMEM((2, 2, highs * pairs, 2 * SHARE, HALF), BF16),
            pltpu.VMEM((2, highs * pairs, 2 * SHARE, HALF), BF16),
            pltpu.VMEM((highs * planes, 2 * SHARE, HALF), BF16),
            pltpu.VMEM((highs * n_y, 2 * SHARE, HALF), BF16),
            pltpu.VMEM((first_share, SHARE, wide), F32),
            pltpu.VMEM((first_share, SHARE, wide), F32),
            pltpu.VMEM((n_y, 2 * SHARE, HALF), BF16),
            pltpu.VMEM((highs * n_y, 2 * SHARE, HALF), BF16),
            pltpu.VMEM((n_z * planes, 2 * SHARE, HALF), BF16),
            dma((8,)),
            dma((planes,)),
            dma((planes,)),
            dma(()),
            dma((2,)),
            dma(()),
            dma(()),
            dma(()),
            dma((bits(planes),)),
            dma(()),
            dma(()),
        ],
        compiler_params=pltpu.CompilerParams(
            collective_id=0, has_side_effects=True, vmem_limit_bytes=40 * 1024 * 1024
        ),
        name="spectral",
    )(*(pltpu.with_memory_space_constraint(value, pltpu.HBM) for value in operands))
    return pl.pallas_call(
        grid_kernel,
        out_shape=jax.ShapeDtypeStruct(field.shape, BF16),
        in_specs=[vmem] * 3,
        out_specs=hbm,
        scratch_shapes=[pltpu.VMEM(field.shape, BF16), dma((planes,))],
        compiler_params=pltpu.CompilerParams(vmem_limit_bytes=40 * 1024 * 1024),
        name="grid",
    )(local, gt, synth)


def solution(mesh):
    return jax.shard_map(
        functools.partial(shards, mesh.shape["gy"], mesh.shape["gz"]),
        mesh=mesh,
        in_specs=(P(None, None, "gy", "gz"), P("gy", "gz", None), P(), P()),
        out_specs=P(None, None, "gy", "gz"),
        check_vma=False,
    )
```

```python
import functools
import math

import jax
import jax.numpy as jnp
import ml_dtypes
import numpy as np
from jax import lax
from jax.experimental import pallas as pl
from jax.experimental.pallas import tpu as pltpu
from jax.sharding import PartitionSpec as P

KY = 32
KZ = 32
BF16 = jnp.bfloat16
F32 = jnp.float32
MESH = pl.DeviceIdType.MESH
SHARE = 8
HALF = 256


def basis(count, length, norm):
    modes = np.arange(count)[:, None]
    spots = np.arange(length)[None, :]
    value = norm * np.cos(np.pi * modes * (spots + 0.5) / length)
    return np.where(modes == 0, value * math.sqrt(0.5), value)


def tables(n_y, n_z, planes, rows, depth, first_share):
    total_rows, total_depth = rows * n_y, depth * n_z
    az = basis(KZ, total_depth, math.sqrt(2.0 / total_depth))
    az = az.astype(np.float32).astype(ml_dtypes.bfloat16).astype(np.float64)
    ax = basis(planes, planes, math.sqrt(2.0 / planes))
    sz = basis(KZ, total_depth, math.sqrt(2.0 / KZ))

    def joint(x_basis, z_basis):
        z = z_basis.reshape(n_z // 2, 2, SHARE, n_z, depth)
        both = np.einsum("ix,hlkdz->dxlhikz", x_basis, z)
        return both.reshape(n_z, planes, planes * KZ, depth).astype(ml_dtypes.bfloat16)

    ay = basis(KY, total_rows, math.sqrt(2.0 / total_rows))
    sy = basis(KY, total_rows, math.sqrt(2.0 / KY))
    blocks = KY // first_share

    def lanes(y_basis):
        parts = y_basis.reshape(blocks, first_share, n_y, rows)
        return np.tile(parts, (1, 1, 1, HALF // rows)).astype(np.float32)

    analysis_y = lanes(ay)
    synth_y = np.ascontiguousarray(np.swapaxes(lanes(0.5 * sy), 1, 2))
    synth = joint(ax, sz).reshape(n_z, planes, 2, planes * KZ // 2, depth)
    analysis = np.ascontiguousarray(np.swapaxes(joint(ax, az), 2, 3))
    return analysis, synth, analysis_y, synth_y


def bits(count):
    assert count & (count - 1) == 0
    return count.bit_length() - 1


def select(shape, row_of, column_of):
    r = row_of(lax.broadcasted_iota(jnp.int32, shape, 0))
    c = column_of(lax.broadcasted_iota(jnp.int32, shape, 1))
    return jnp.where(r == c, 1.0, 0.0).astype(F32)


def spectral_kernel(
    n_y, n_z, field, a_tab, b_tab, weight, point, bias, ay_tab, sy_tab, local, gt_out, b_out,
    f_v, a_v, w_v, p_v, bias_s, bias_v, ay_v, sy_v, e1, e2, spread, kron,
    part, got1, owned, got2, u_v, m_v, tout, got3, modes,
    load_sem, send1, recv1, send2, recv2, send3, recv3, send4, recv4,
):
    me_y, me_z = lax.axis_index("gy"), lax.axis_index("gz")
    chans, planes, rows, depth = f_v.shape
    pairs = planes // 2
    group = n_y // planes
    highs = n_z // 2
    high, low = lax.div(me_z, 2), lax.rem(me_z, 2)
    near = high * 2 + 1 - low
    first_share = w_v.shape[0]
    mine, place = lax.div(me_y, group), lax.rem(me_y, group)
    block = place if first_share < KY else 0
    others = [
        (d, t, u) for d in range(planes) for t in range(group) for u in range(highs)
    ][1:]

    def flip(index, mask):
        for k in range(bits(planes)):
            if mask >> k & 1:
                bit = lax.rem(lax.div(index, 1 << k), 2)
                index = index + (1 << k) * (1 - 2 * bit)
        return index

    def at(d, t):
        return flip(mine, d) * group + lax.rem(place + t, group)

    def came(d, t):
        return flip(mine, d) * group + lax.rem(place - t + group, group)

    def high_at(u):
        return lax.rem(high + u, highs)

    def arrived(blocks, semaphore):
        pltpu.make_async_copy(blocks, blocks, semaphore).wait()

    barrier = pltpu.get_barrier_semaphore()
    pl.semaphore_signal(barrier, inc=1, device_id=(me_y, near), device_id_type=MESH)
    for d, t, u in others:
        pl.semaphore_signal(
            barrier, inc=1, device_id=(at(d, t), high_at(u) * 2 + low), device_id_type=MESH
        )

    half = planes // 2
    side = planes * KZ // 2
    loads = []
    for h in range(2):
        of = pl.ds(h * half, half)
        loads.append(pltpu.make_async_copy(a_tab.at[me_z, of], a_v.at[of], load_sem.at[2 * h]))
        loads.append(
            pltpu.make_async_copy(field.at[:, of], f_v.at[:, of], load_sem.at[2 * h + 1])
        )
    loads += [
        pltpu.make_async_copy(weight, w_v, load_sem.at[4]),
        pltpu.make_async_copy(point, p_v, load_sem.at[5]),
        pltpu.make_async_copy(bias, bias_s, load_sem.at[6]),
        pltpu.make_async_copy(ay_tab.at[block], ay_v, load_sem.at[7]),
        pltpu.make_async_copy(sy_tab.at[block], sy_v, load_sem.at[8]),
        pltpu.make_async_copy(b_tab.at[me_z, :, low], b_out.at[:, 0:side], load_sem.at[9]),
        pltpu.make_async_copy(
            b_tab.at[me_z, :, 1 - low], b_out.at[:, side:2 * side], load_sem.at[10]
        ),
    ]
    for load in loads:
        load.start()

    e1[...] = select(
        e1.shape, lambda r: r >> bits(rows), lambda c: c >> bits(chans)
    ).astype(BF16)

    pair_order = range(pairs - 1, -1, -1)
    total = None
    for h in range(2):
        loads[2 * h].wait()
        loads[2 * h + 1].wait()
        planes_of = range(h * half, (h + 1) * half)
        grid = jnp.concatenate(
            [f_v[:, x].reshape(chans * rows, depth) for x in planes_of], axis=1
        )
        table = a_v[h * half:(h + 1) * half].reshape(half * depth, planes * KZ)
        term = jnp.dot(grid, table, preferred_element_type=F32)
        total = term if total is None else total + term
    for h in range(2):
        turned = total[h * HALF:(h + 1) * HALF].T
        part[h] = turned.reshape(2, highs * pairs, 2 * SHARE, HALF).astype(BF16)
        if h == 0:
            pl.semaphore_wait(barrier, 1 + len(others))
        pltpu.make_async_remote_copy(
            src_ref=part.at[h, 1 - low],
            dst_ref=got1.at[h],
            send_sem=send1,
            recv_sem=recv1.at[h],
            device_id=(me_y, near),
            device_id_type=MESH,
        ).start()

    e2[...] = select(
        e2.shape, lambda r: r & (chans - 1), lambda c: c >> bits(rows)
    ).astype(BF16)
    for h in range(2):
        arrived(got1.at[h], recv1.at[h])
    for p in pair_order:
        ip = lax.div(flip(mine, 2 * p), 2)
        for u in range(highs):
            slot = high_at(u) * pairs + ip
            sums = []
            for h in range(2):
                sums.append(part[h, low, slot].astype(F32) + got1[h, slot].astype(F32))
            for odd in range(2):
                of = slice(odd * SHARE, (odd + 1) * SHARE)
                owned[high_at(u) * planes + ip * 2 + odd] = jnp.concatenate(
                    [sums[0][of], sums[1][of]], axis=0
                ).astype(BF16)
        for d in (2 * p + 1, 2 * p):
            for t in range(group):
                for u in range(highs):
                    if d == 0 and t == 0 and u == 0:
                        continue
                    pltpu.make_async_remote_copy(
                        src_ref=owned.at[high_at(u) * planes + flip(mine, d)],
                        dst_ref=got2.at[high * n_y + me_y],
                        send_sem=send2,
                        recv_sem=recv2,
                        device_id=(at(d, t), high_at(u) * 2 + low),
                        device_id_type=MESH,
                    ).start()
    got2[high * n_y + me_y] = owned[high * planes + mine]

    spread[...] = select(spread.shape, lambda r: r >> bits(rows), lambda c: c).astype(BF16)

    loads[5].wait()
    wide = lax.dot_general(
        spread[...], p_v[...], (((1,), (1,)), ((), ())), preferred_element_type=F32
    ).astype(BF16)
    wide = lax.dot_general(
        wide, spread[...], (((1,), (1,)), ((), ())), preferred_element_type=F32
    )
    same = select(wide.shape, lambda r: r & (rows - 1), lambda c: c & (rows - 1))
    kron[...] = (wide * (0.5 * same)).astype(BF16)
    loads[6].wait()
    for o in range(chans):
        bias_v[o * rows:(o + 1) * rows, :] = jnp.full((rows, depth), 0.5 * bias_s[o], F32)

    def pointwise(x):
        grid = f_v[:, x].reshape(chans * rows, depth)
        value = jnp.dot(kron[...], grid, preferred_element_type=F32)
        local[x] = value + bias_v[...]

    for x in range(4):
        pointwise(x)

    for load in (loads[4], loads[7], loads[8]):
        load.wait()
    arrived(got2.at[0:len(others)], recv2)
    for h in range(2):
        pieces = []
        for s in range(n_y):
            total = got2[s].astype(F32)
            for u in range(1, highs):
                total += got2[u * n_y + s].astype(F32)
            pieces.append(total[h * SHARE:(h + 1) * SHARE])
        for j in range(first_share):
            total = pieces[0] * ay_v[j, 0:1, :]
            for s in range(1, n_y):
                total += pieces[s] * ay_v[j, s:s + 1, :]
            u_v[j, :, h * HALF:(h + 1) * HALF] = total

    mode_rows = first_share * SHARE
    spectrum = jnp.dot(
        u_v[...].reshape(mode_rows, 2 * HALF).astype(BF16), e1[...], preferred_element_type=F32
    )
    terms = spectrum * w_v[...].astype(F32).reshape(mode_rows, chans * chans)
    mixed = jnp.dot(terms.astype(BF16), e2[...], preferred_element_type=F32)
    m_v[...] = mixed.reshape(first_share, SHARE, 2 * HALF)

    sets = [range(1 << k, 2 << k) for k in range(bits(planes) - 1, 0, -1)] + [range(2)]
    landing = modes if group == 1 else got3

    def land(index, sender):
        start = low * highs * planes if group == 1 else 0
        return start + index * n_y + sender

    for c, members in enumerate(sets):
        places = [(d, t) for d in members[::-1] for t in range(group - 1, -1, -1)]
        for index in range(0, len(places), 4):
            batch = places[index:index + 4]
            sums = [[None, None] for _ in batch]
            for j in range(first_share):
                for h in range(2):
                    mode = m_v[j, :, h * HALF:(h + 1) * HALF]
                    for b, (d, t) in enumerate(batch):
                        term = mode * sy_v[at(d, t), j:j + 1, :]
                        sums[b][h] = term if j == 0 else sums[b][h] + term
            for b, (d, t) in enumerate(batch):
                target = at(d, t)
                tout[target] = jnp.concatenate(sums[b], axis=0).astype(BF16)
                for u in range(highs):
                    if d == 0 and t == 0 and u == 0:
                        landing[land(high, me_y)] = tout[target]
                        continue
                    pltpu.make_async_remote_copy(
                        src_ref=tout.at[target],
                        dst_ref=landing.at[land(high, me_y)],
                        send_sem=send3,
                        recv_sem=recv3.at[c],
                        device_id=(target, high_at(u) * 2 + low),
                        device_id_type=MESH,
                    ).start()

    for x in range(4, planes):
        pointwise(x)
    for load in loads[9:]:
        load.wait()

    for c, members in enumerate(sets):
        count = len(members) * group * highs - (1 if 0 in members else 0)
        arrived(landing.at[0:count], recv3.at[c])
        size = len(members)
        first = lax.div(flip(mine, members[0]), size) * size
        for index in range(highs):
            start = (low * highs + index) * planes
            if group > 1:
                for d in members:
                    total = landing[land(index, came(d, 0))].astype(F32)
                    for t in range(1, group):
                        total += landing[land(index, came(d, t))].astype(F32)
                    modes[start + flip(mine, d)] = total.astype(BF16)
            pltpu.make_async_remote_copy(
                src_ref=modes.at[pl.ds(start + first, size)],
                dst_ref=modes.at[pl.ds(start + first, size)],
                send_sem=send4,
                recv_sem=recv4,
                device_id=(me_y, near),
                device_id_type=MESH,
            ).start()

    def turn(part_of, start):
        value = modes[pl.ds(start, highs * planes)].astype(F32)
        for h in range(2):
            one = value[:, h * SHARE:(h + 1) * SHARE, :].reshape(side, HALF)
            gt_out[h * HALF:(h + 1) * HALF, part_of * side:(part_of + 1) * side] = one.T.astype(BF16)

    turn(0, low * highs * planes)
    arrived(modes.at[0:highs * planes], recv4)
    turn(1, (1 - low) * highs * planes)
    arrived(got1, send1)
    arrived(got2.at[0:len(others)], send2)
    arrived(got2.at[0:len(others)], send3)
    arrived(modes.at[0:highs * planes], send4)


def grid_kernel(local, gt, synth, out, o_v, out_sem):
    planes, _, depth = local.shape
    chans, _, rows, _ = o_v.shape
    stores = []
    scale = math.sqrt(2.0 / math.pi)
    for x in range(planes):
        value = local[x] + jnp.dot(gt[...], synth[x], preferred_element_type=F32)
        inner = value * (2.0 * scale + (8.0 * scale * 0.044715) * (value * value))
        value += value * jnp.tanh(inner)
        o_v[:, x] = value.astype(BF16).reshape(chans, rows, depth)
        store = pltpu.make_async_copy(o_v.at[:, x], out.at[:, x], out_sem.at[x])
        store.start()
        stores.append(store)
    for store in stores:
        store.wait()


def shards(n_y, n_z, field, spectral_weight, point_weight, bias):
    chans, planes, rows, depth = field.shape
    first_share, depth_share = spectral_weight.shape[:2]
    assert depth_share == SHARE and chans * rows == 2 * HALF and first_share <= KY
    assert n_y % planes == 0 and depth_share * n_z == KZ and planes % 2 == 0 and n_z % 2 == 0
    a_tab, b_tab, ay_tab, sy_tab = tables(n_y, n_z, planes, rows, depth, first_share)
    pairs, highs = planes // 2, n_z // 2
    vmem = pl.BlockSpec(memory_space=pltpu.VMEM)
    hbm = pl.BlockSpec(memory_space=pltpu.HBM)
    wide = 2 * HALF
    dma = pltpu.SemaphoreType.DMA
    operands = [field, a_tab, b_tab, spectral_weight, point_weight, bias, ay_tab, sy_tab]
    local, gt, synth = pl.pallas_call(
        functools.partial(spectral_kernel, n_y, n_z),
        out_shape=(
            pltpu.VMEM((planes, wide, depth), F32),
            pltpu.VMEM((wide, planes * KZ), BF16),
            pltpu.VMEM((planes, planes * KZ, depth), BF16),
        ),
        in_specs=[hbm] * len(operands),
        out_specs=(vmem, vmem, vmem),
        scratch_shapes=[
            pltpu.VMEM(field.shape, BF16),
            pltpu.VMEM(a_tab.shape[1:], BF16),
            pltpu.VMEM(spectral_weight.shape, BF16),
            pltpu.VMEM(point_weight.shape, BF16),
            pltpu.SMEM(bias.shape, F32),
            pltpu.VMEM((wide, depth), F32),
            pltpu.VMEM(ay_tab.shape[1:], F32),
            pltpu.VMEM(sy_tab.shape[1:], F32),
            pltpu.VMEM((wide, chans * chans), BF16),
            pltpu.VMEM((chans * chans, wide), BF16),
            pltpu.VMEM((wide, chans), BF16),
            pltpu.VMEM((wide, wide), BF16),
            pltpu.VMEM((2, 2, highs * pairs, 2 * SHARE, HALF), BF16),
            pltpu.VMEM((2, highs * pairs, 2 * SHARE, HALF), BF16),
            pltpu.VMEM((highs * planes, 2 * SHARE, HALF), BF16),
            pltpu.VMEM((highs * n_y, 2 * SHARE, HALF), BF16),
            pltpu.VMEM((first_share, SHARE, wide), F32),
            pltpu.VMEM((first_share, SHARE, wide), F32),
            pltpu.VMEM((n_y, 2 * SHARE, HALF), BF16),
            pltpu.VMEM((highs * n_y, 2 * SHARE, HALF), BF16),
            pltpu.VMEM((n_z * planes, 2 * SHARE, HALF), BF16),
            dma((11,)),
            dma(()),
            dma((2,)),
            dma(()),
            dma(()),
            dma(()),
            dma((bits(planes),)),
            dma(()),
            dma(()),
        ],
        compiler_params=pltpu.CompilerParams(
            collective_id=0, has_side_effects=True, vmem_limit_bytes=40 * 1024 * 1024
        ),
        name="spectral",
    )(*(pltpu.with_memory_space_constraint(value, pltpu.HBM) for value in operands))
    return pl.pallas_call(
        grid_kernel,
        out_shape=jax.ShapeDtypeStruct(field.shape, BF16),
        in_specs=[vmem] * 3,
        out_specs=hbm,
        scratch_shapes=[pltpu.VMEM(field.shape, BF16), dma((planes,))],
        compiler_params=pltpu.CompilerParams(vmem_limit_bytes=40 * 1024 * 1024),
        name="grid",
    )(local, gt, synth)


def solution(mesh):
    return jax.shard_map(
        functools.partial(shards, mesh.shape["gy"], mesh.shape["gz"]),
        mesh=mesh,
        in_specs=(P(None, None, "gy", "gz"), P("gy", "gz", None), P(), P()),
        out_specs=P(None, None, "gy", "gz"),
        check_vma=False,
    )
```

```python
import functools
import math

import jax
import jax.numpy as jnp
import ml_dtypes
import numpy as np
from jax import lax
from jax.experimental import pallas as pl
from jax.experimental.pallas import tpu as pltpu
from jax.sharding import PartitionSpec as P

KY = 32
KZ = 32
BF16 = jnp.bfloat16
F32 = jnp.float32
MESH = pl.DeviceIdType.MESH
SHARE = 8
HALF = 256
LANES = 128


def basis(count, length, norm):
    modes = np.arange(count)[:, None]
    spots = np.arange(length)[None, :]
    value = norm * np.cos(np.pi * modes * (spots + 0.5) / length)
    return np.where(modes == 0, value * math.sqrt(0.5), value)


def tables(n_y, n_z, planes, rows, depth, first_share):
    total_rows, total_depth = rows * n_y, depth * n_z
    az = basis(KZ, total_depth, math.sqrt(2.0 / total_depth))
    az = az.astype(np.float32).astype(ml_dtypes.bfloat16).astype(np.float64)
    ax = basis(planes, planes, math.sqrt(2.0 / planes))
    sz = basis(KZ, total_depth, math.sqrt(2.0 / KZ))

    def joint(x_basis, z_basis):
        z = z_basis.reshape(n_z // 2, 2, SHARE, n_z, depth)
        both = np.einsum("ix,hlkdz->dxlhikz", x_basis, z)
        return both.reshape(n_z, planes, planes * KZ, depth).astype(ml_dtypes.bfloat16)

    ay = basis(KY, total_rows, math.sqrt(2.0 / total_rows))
    sy = basis(KY, total_rows, math.sqrt(2.0 / KY))
    blocks = KY // first_share

    def lanes(y_basis):
        parts = y_basis.reshape(blocks, first_share, n_y, rows)
        return np.tile(parts, (1, 1, 1, HALF // rows)).astype(np.float32)

    analysis_y = lanes(ay)
    synth_y = np.ascontiguousarray(np.swapaxes(lanes(0.5 * sy), 1, 2))
    synth = joint(ax, sz).reshape(n_z, planes, 2, planes * KZ // 2, depth)
    analysis = np.ascontiguousarray(np.swapaxes(joint(ax, az), 2, 3))
    return analysis, synth, analysis_y, synth_y


def bits(count):
    assert count & (count - 1) == 0
    return count.bit_length() - 1


def select(shape, row_of, column_of):
    r = row_of(lax.broadcasted_iota(jnp.int32, shape, 0))
    c = column_of(lax.broadcasted_iota(jnp.int32, shape, 1))
    return jnp.where(r == c, 1.0, 0.0).astype(F32)


def spectral_kernel(
    n_y, n_z, field, a_tab, b_tab, weight, point, bias, ay_tab, sy_tab, local, gt_out, b_out,
    f_v, a_v, w_v, p_v, bias_s, bias_v, ay_v, sy_v, e1, e2, spread, kron,
    part, got1, owned, got2, u_v, t_v, m_v, tout, got3, modes,
    load_sem, send1, recv1, send2, recv2, send3, recv3, send4, recv4,
):
    me_y, me_z = lax.axis_index("gy"), lax.axis_index("gz")
    chans, planes, rows, depth = f_v.shape
    group = n_y // planes
    highs = n_z // 2
    high, low = lax.div(me_z, 2), lax.rem(me_z, 2)
    near = high * 2 + 1 - low
    first_share = w_v.shape[0]
    mine, place = lax.div(me_y, group), lax.rem(me_y, group)
    block = place if first_share < KY else 0
    others = [
        (d, t, u) for d in range(planes) for t in range(group) for u in range(highs)
    ][1:]

    def flip(index, mask):
        for k in range(bits(planes)):
            if mask >> k & 1:
                bit = lax.rem(lax.div(index, 1 << k), 2)
                index = index + (1 << k) * (1 - 2 * bit)
        return index

    def at(d, t):
        return flip(mine, d) * group + lax.rem(place + t, group)

    def came(d, t):
        return flip(mine, d) * group + lax.rem(place - t + group, group)

    def high_at(u):
        return lax.rem(high + u, highs)

    def arrived(blocks, semaphore):
        pltpu.make_async_copy(blocks, blocks, semaphore).wait()

    barrier = pltpu.get_barrier_semaphore()
    pl.semaphore_signal(barrier, inc=1, device_id=(me_y, near), device_id_type=MESH)
    for d, t, u in others:
        pl.semaphore_signal(
            barrier, inc=1, device_id=(at(d, t), high_at(u) * 2 + low), device_id_type=MESH
        )

    half = chans // 2
    side = planes * KZ // 2
    loads = [
        pltpu.make_async_copy(a_tab.at[me_z], a_v, load_sem.at[0]),
        pltpu.make_async_copy(field.at[0:half], f_v.at[0:half], load_sem.at[1]),
        pltpu.make_async_copy(field.at[half:chans], f_v.at[half:chans], load_sem.at[2]),
        pltpu.make_async_copy(weight, w_v, load_sem.at[3]),
        pltpu.make_async_copy(point, p_v, load_sem.at[4]),
        pltpu.make_async_copy(bias, bias_s, load_sem.at[5]),
        pltpu.make_async_copy(ay_tab.at[block], ay_v, load_sem.at[6]),
        pltpu.make_async_copy(sy_tab.at[block], sy_v, load_sem.at[7]),
        pltpu.make_async_copy(b_tab.at[me_z, :, low], b_out.at[:, 0:side], load_sem.at[8]),
        pltpu.make_async_copy(
            b_tab.at[me_z, :, 1 - low], b_out.at[:, side:2 * side], load_sem.at[9]
        ),
    ]
    for load in loads:
        load.start()

    e1[...] = select(
        e1.shape, lambda r: r >> bits(rows), lambda c: c >> bits(chans)
    ).astype(BF16)

    def stacked(value):
        return jnp.concatenate([value[..., :LANES], value[..., LANES:]], axis=-2)

    table = a_v.reshape(planes * depth, planes * KZ)
    loads[0].wait()
    for h in range(2):
        loads[1 + h].wait()
        grid = jnp.concatenate(
            [f_v[h * half:(h + 1) * half, x].reshape(HALF, depth) for x in range(planes)], axis=1
        )
        turned = jnp.dot(grid, table[...], preferred_element_type=F32).T
        turned = turned.reshape(2, highs * planes, SHARE, HALF)
        part[h] = stacked(turned).astype(BF16)
        if h == 0:
            pl.semaphore_wait(barrier, 1 + len(others))
        pltpu.make_async_remote_copy(
            src_ref=part.at[h, 1 - low],
            dst_ref=got1.at[h],
            send_sem=send1,
            recv_sem=recv1.at[h],
            device_id=(me_y, near),
            device_id_type=MESH,
        ).start()

    for h in range(2):
        arrived(got1.at[h], recv1.at[h])
        owned[h] = (part[h, low].astype(F32) + got1[h].astype(F32)).astype(BF16)
        for d, t, u in others[::-1]:
            pltpu.make_async_remote_copy(
                src_ref=owned.at[h, high_at(u) * planes + flip(mine, d)],
                dst_ref=got2.at[h, high * n_y + me_y],
                send_sem=send2.at[h],
                recv_sem=recv2.at[h],
                device_id=(at(d, t), high_at(u) * 2 + low),
                device_id_type=MESH,
            ).start()
        got2[h, high * n_y + me_y] = owned[h, high * planes + mine]

    e2[...] = select(
        e2.shape, lambda r: r & (chans - 1), lambda c: c >> bits(rows)
    ).astype(BF16)
    spread[...] = select(spread.shape, lambda r: r >> bits(rows), lambda c: c).astype(BF16)

    loads[4].wait()
    wide = lax.dot_general(
        spread[...], p_v[...], (((1,), (1,)), ((), ())), preferred_element_type=F32
    ).astype(BF16)
    wide = lax.dot_general(
        wide, spread[...], (((1,), (1,)), ((), ())), preferred_element_type=F32
    )
    same = select(wide.shape, lambda r: r & (rows - 1), lambda c: c & (rows - 1))
    kron[...] = (wide * (0.5 * same)).astype(BF16)
    loads[5].wait()
    for o in range(chans):
        bias_v[o * rows:(o + 1) * rows, :] = jnp.full((rows, depth), 0.5 * bias_s[o], F32)

    def pointwise(x):
        grid = f_v[:, x].reshape(chans * rows, depth)
        value = jnp.dot(kron[...], grid, preferred_element_type=F32)
        local[x] = value + bias_v[...]

    for x in range(4):
        pointwise(x)

    for load in (loads[3], loads[6], loads[7]):
        load.wait()
    mode_rows = first_share * SHARE
    most = len(others)
    for h in range(2):
        arrived(got2.at[h, 0:most], recv2.at[h])
        pieces = []
        for s in range(n_y):
            total = got2[h, s].astype(F32)
            for u in range(1, highs):
                total += got2[h, u * n_y + s].astype(F32)
            pieces.append(total)
        for j in range(first_share):
            total = pieces[0] * ay_v[j, 0:1, :LANES]
            for s in range(1, n_y):
                total += pieces[s] * ay_v[j, s:s + 1, :LANES]
            u_v[h, j, :, :LANES] = total[:SHARE]
            u_v[h, j, :, LANES:] = total[SHARE:]
        spectrum = jnp.dot(
            u_v[h].reshape(mode_rows, HALF).astype(BF16), e1[...], preferred_element_type=F32
        )
        wide = half * chans
        weights = w_v[:, :, h * wide:(h + 1) * wide].astype(F32).reshape(mode_rows, wide)
        terms = spectrum * weights
        total = terms[:, :LANES]
        for lane in range(LANES, wide, LANES):
            total += terms[:, lane:lane + LANES]
        t_v[...] = total if h == 0 else t_v[...] + total

    landing = modes if group == 1 else got3

    def land(index, sender):
        start = low * highs * planes if group == 1 else 0
        return start + index * n_y + sender

    places = [(d, t) for d in range(planes) for t in range(group)][::-1]
    for g in range(2):
        mixed = jnp.dot(
            t_v[...].astype(BF16), e2[:, g * HALF:(g + 1) * HALF], preferred_element_type=F32
        )
        m_v[g] = mixed.reshape(first_share, SHARE, HALF)
        for index in range(0, len(places), 4):
            batch = places[index:index + 4]
            sums = [None] * len(batch)
            for j in range(first_share):
                mode = m_v[g, j]
                for b, (d, t) in enumerate(batch):
                    term = mode * sy_v[at(d, t), j:j + 1, :]
                    sums[b] = term if j == 0 else sums[b] + term
            for b, (d, t) in enumerate(batch):
                target = at(d, t)
                tout[g, target] = stacked(sums[b]).astype(BF16)
                for u in range(highs):
                    if d == 0 and t == 0 and u == 0:
                        landing[g, land(high, me_y)] = tout[g, target]
                        continue
                    pltpu.make_async_remote_copy(
                        src_ref=tout.at[g, target],
                        dst_ref=landing.at[g, land(high, me_y)],
                        send_sem=send3.at[g],
                        recv_sem=recv3.at[g],
                        device_id=(target, high_at(u) * 2 + low),
                        device_id_type=MESH,
                    ).start()

    for x in range(4, planes):
        pointwise(x)
    for load in loads[8:]:
        load.wait()

    block_of = pl.ds(low * highs * planes, highs * planes)
    for g in range(2):
        arrived(landing.at[g, 0:most], recv3.at[g])
        if group > 1:
            for index in range(highs):
                for i in range(planes):
                    total = got3[g, index * n_y + i * group].astype(F32)
                    for t in range(1, group):
                        total += got3[g, index * n_y + i * group + t].astype(F32)
                    modes[g, (low * highs + index) * planes + i] = total.astype(BF16)
        pltpu.make_async_remote_copy(
            src_ref=modes.at[g, block_of],
            dst_ref=modes.at[g, block_of],
            send_sem=send4.at[g],
            recv_sem=recv4.at[g],
            device_id=(me_y, near),
            device_id_type=MESH,
        ).start()

    def turn(g, part_of, start):
        value = modes[g, pl.ds(start, highs * planes)].astype(F32)
        for q in range(2):
            one = value[:, q * SHARE:(q + 1) * SHARE, :].reshape(side, LANES)
            first = g * HALF + q * LANES
            gt_out[first:first + LANES, part_of * side:(part_of + 1) * side] = one.T.astype(BF16)

    for g in range(2):
        turn(g, 0, low * highs * planes)
    for g in range(2):
        arrived(modes.at[g, 0:highs * planes], recv4.at[g])
        turn(g, 1, (1 - low) * highs * planes)
    arrived(got1, send1)
    for g in range(2):
        arrived(got2.at[g, 0:most], send2.at[g])
        arrived(got2.at[g, 0:most], send3.at[g])
        arrived(modes.at[g, 0:highs * planes], send4.at[g])


def grid_kernel(local, gt, synth, out, o_v, out_sem):
    planes, _, depth = local.shape
    chans, _, rows, _ = o_v.shape
    stores = []
    scale = math.sqrt(2.0 / math.pi)
    for x in range(planes):
        value = local[x] + jnp.dot(gt[...], synth[x], preferred_element_type=F32)
        inner = value * (2.0 * scale + (8.0 * scale * 0.044715) * (value * value))
        value += value * jnp.tanh(inner)
        o_v[:, x] = value.astype(BF16).reshape(chans, rows, depth)
        store = pltpu.make_async_copy(o_v.at[:, x], out.at[:, x], out_sem.at[x])
        store.start()
        stores.append(store)
    for store in stores:
        store.wait()


def shards(n_y, n_z, field, spectral_weight, point_weight, bias):
    chans, planes, rows, depth = field.shape
    first_share, depth_share = spectral_weight.shape[:2]
    assert depth_share == SHARE and chans * rows == 2 * HALF and first_share <= KY
    assert n_y % planes == 0 and depth_share * n_z == KZ and planes % 2 == 0 and n_z % 2 == 0
    a_tab, b_tab, ay_tab, sy_tab = tables(n_y, n_z, planes, rows, depth, first_share)
    highs = n_z // 2
    vmem = pl.BlockSpec(memory_space=pltpu.VMEM)
    hbm = pl.BlockSpec(memory_space=pltpu.HBM)
    wide = 2 * HALF
    dma = pltpu.SemaphoreType.DMA
    operands = [field, a_tab, b_tab, spectral_weight, point_weight, bias, ay_tab, sy_tab]
    local, gt, synth = pl.pallas_call(
        functools.partial(spectral_kernel, n_y, n_z),
        out_shape=(
            pltpu.VMEM((planes, wide, depth), F32),
            pltpu.VMEM((wide, planes * KZ), BF16),
            pltpu.VMEM((planes, planes * KZ, depth), BF16),
        ),
        in_specs=[hbm] * len(operands),
        out_specs=(vmem, vmem, vmem),
        scratch_shapes=[
            pltpu.VMEM(field.shape, BF16),
            pltpu.VMEM(a_tab.shape[1:], BF16),
            pltpu.VMEM(spectral_weight.shape, BF16),
            pltpu.VMEM(point_weight.shape, BF16),
            pltpu.SMEM(bias.shape, F32),
            pltpu.VMEM((wide, depth), F32),
            pltpu.VMEM(ay_tab.shape[1:], F32),
            pltpu.VMEM(sy_tab.shape[1:], F32),
            pltpu.VMEM((HALF, chans * chans // 2), BF16),
            pltpu.VMEM((LANES, wide), BF16),
            pltpu.VMEM((wide, chans), BF16),
            pltpu.VMEM((wide, wide), BF16),
            pltpu.VMEM((2, 2, highs * planes, 2 * SHARE, LANES), BF16),
            pltpu.VMEM((2, highs * planes, 2 * SHARE, LANES), BF16),
            pltpu.VMEM((2, highs * planes, 2 * SHARE, LANES), BF16),
            pltpu.VMEM((2, highs * n_y, 2 * SHARE, LANES), BF16),
            pltpu.VMEM((2, first_share, SHARE, HALF), F32),
            pltpu.VMEM((first_share * SHARE, LANES), F32),
            pltpu.VMEM((2, first_share, SHARE, HALF), F32),
            pltpu.VMEM((2, n_y, 2 * SHARE, LANES), BF16),
            pltpu.VMEM((2, highs * n_y, 2 * SHARE, LANES), BF16),
            pltpu.VMEM((2, 2 * highs * planes, 2 * SHARE, LANES), BF16),
            dma((10,)),
            dma(()),
            dma((2,)),
            dma((2,)),
            dma((2,)),
            dma((2,)),
            dma((2,)),
            dma((2,)),
            dma((2,)),
        ],
        compiler_params=pltpu.CompilerParams(
            collective_id=0, has_side_effects=True, vmem_limit_bytes=40 * 1024 * 1024
        ),
        name="spectral",
    )(*(pltpu.with_memory_space_constraint(value, pltpu.HBM) for value in operands))
    return pl.pallas_call(
        grid_kernel,
        out_shape=jax.ShapeDtypeStruct(field.shape, BF16),
        in_specs=[vmem] * 3,
        out_specs=hbm,
        scratch_shapes=[pltpu.VMEM(field.shape, BF16), dma((planes,))],
        compiler_params=pltpu.CompilerParams(vmem_limit_bytes=40 * 1024 * 1024),
        name="grid",
    )(local, gt, synth)


def solution(mesh):
    return jax.shard_map(
        functools.partial(shards, mesh.shape["gy"], mesh.shape["gz"]),
        mesh=mesh,
        in_specs=(P(None, None, "gy", "gz"), P("gy", "gz", None), P(), P()),
        out_specs=P(None, None, "gy", "gz"),
        check_vma=False,
    )
```

```python
import functools
import math

import jax
import jax.numpy as jnp
import ml_dtypes
import numpy as np
from jax import lax
from jax.experimental import pallas as pl
from jax.experimental.pallas import tpu as pltpu
from jax.sharding import PartitionSpec as P

KY = 32
KZ = 32
BF16 = jnp.bfloat16
F32 = jnp.float32
MESH = pl.DeviceIdType.MESH
SHARE = 8
HALF = 256
LANES = 128


def basis(count, length, norm):
    modes = np.arange(count)[:, None]
    spots = np.arange(length)[None, :]
    value = norm * np.cos(np.pi * modes * (spots + 0.5) / length)
    return np.where(modes == 0, value * math.sqrt(0.5), value)


def tables(n_y, n_z, planes, rows, depth, first_share):
    total_rows, total_depth = rows * n_y, depth * n_z
    az = basis(KZ, total_depth, math.sqrt(2.0 / total_depth))
    az = az.astype(np.float32).astype(ml_dtypes.bfloat16).astype(np.float64)
    ax = basis(planes, planes, math.sqrt(2.0 / planes))
    sz = basis(KZ, total_depth, math.sqrt(2.0 / KZ))

    def joint(x_basis, z_basis):
        z = z_basis.reshape(n_z // 2, 2, SHARE, n_z, depth)
        both = np.einsum("ix,hlkdz->dxlhikz", x_basis, z)
        return both.reshape(n_z, planes, planes * KZ, depth).astype(ml_dtypes.bfloat16)

    ay = basis(KY, total_rows, math.sqrt(2.0 / total_rows))
    sy = basis(KY, total_rows, math.sqrt(2.0 / KY))
    blocks = KY // first_share

    def lanes(y_basis):
        parts = y_basis.reshape(blocks, first_share, n_y, rows)
        return np.tile(parts, (1, 1, 1, HALF // rows)).astype(np.float32)

    analysis_y = lanes(ay)
    synth_y = np.ascontiguousarray(np.swapaxes(lanes(0.5 * sy), 1, 2))
    synth = joint(ax, sz).reshape(n_z, planes, 2, planes * KZ // 2, depth)
    analysis = np.ascontiguousarray(np.swapaxes(joint(ax, az), 2, 3))
    return analysis, synth, analysis_y, synth_y


def bits(count):
    assert count & (count - 1) == 0
    return count.bit_length() - 1


def select(shape, row_of, column_of):
    r = row_of(lax.broadcasted_iota(jnp.int32, shape, 0))
    c = column_of(lax.broadcasted_iota(jnp.int32, shape, 1))
    return jnp.where(r == c, 1.0, 0.0).astype(F32)


def spectral_kernel(
    n_y, n_z, field, a_tab, b_tab, weight, point, bias, ay_tab, sy_tab, local, gt_out, b_out,
    f_v, a_v, w_v, p_v, bias_s, bias_v, ay_v, sy_v, e1, e2, spread, kron,
    part, got1, owned, got2, u_v, t_v, m_v, tout, got3, modes,
    load_sem, send1, recv1, send2, recv2, send3, recv3, send4, recv4,
):
    me_y, me_z = lax.axis_index("gy"), lax.axis_index("gz")
    chans, planes, rows, depth = f_v.shape
    group = n_y // planes
    highs = n_z // 2
    high, low = lax.div(me_z, 2), lax.rem(me_z, 2)
    near = high * 2 + 1 - low
    first_share = w_v.shape[0]
    mine, place = lax.div(me_y, group), lax.rem(me_y, group)
    block = place if first_share < KY else 0
    others = [
        (d, t, u) for d in range(planes) for t in range(group) for u in range(highs)
    ][1:]

    def flip(index, mask):
        for k in range(bits(planes)):
            if mask >> k & 1:
                bit = lax.rem(lax.div(index, 1 << k), 2)
                index = index + (1 << k) * (1 - 2 * bit)
        return index

    def at(d, t):
        return flip(mine, d) * group + lax.rem(place + t, group)

    def came(d, t):
        return flip(mine, d) * group + lax.rem(place - t + group, group)

    def high_at(u):
        return lax.rem(high + u, highs)

    def arrived(blocks, semaphore):
        pltpu.make_async_copy(blocks, blocks, semaphore).wait()

    barrier = pltpu.get_barrier_semaphore()
    pl.semaphore_signal(barrier, inc=1, device_id=(me_y, near), device_id_type=MESH)
    for d, t, u in others:
        pl.semaphore_signal(
            barrier, inc=1, device_id=(at(d, t), high_at(u) * 2 + low), device_id_type=MESH
        )

    half = chans // 2
    side = planes * KZ // 2
    early = [
        pltpu.make_async_copy(point, p_v, load_sem.at[4]),
        pltpu.make_async_copy(bias, bias_s, load_sem.at[5]),
    ]
    loads = [
        pltpu.make_async_copy(a_tab.at[me_z], a_v, load_sem.at[0]),
        pltpu.make_async_copy(field.at[0:half], f_v.at[0:half], load_sem.at[1]),
        pltpu.make_async_copy(field.at[half:chans], f_v.at[half:chans], load_sem.at[2]),
        pltpu.make_async_copy(weight, w_v, load_sem.at[3]),
        pltpu.make_async_copy(ay_tab.at[block], ay_v, load_sem.at[6]),
        pltpu.make_async_copy(sy_tab.at[block], sy_v, load_sem.at[7]),
        pltpu.make_async_copy(b_tab.at[me_z, :, low], b_out.at[:, 0:side], load_sem.at[8]),
        pltpu.make_async_copy(
            b_tab.at[me_z, :, 1 - low], b_out.at[:, side:2 * side], load_sem.at[9]
        ),
    ]
    for load in early + loads:
        load.start()

    e1[...] = select(
        e1.shape, lambda r: r >> bits(rows), lambda c: c >> bits(chans)
    ).astype(BF16)

    e2[...] = select(
        e2.shape, lambda r: r & (chans - 1), lambda c: c >> bits(rows)
    ).astype(BF16)
    spread[...] = select(spread.shape, lambda r: r >> bits(rows), lambda c: c).astype(BF16)

    early[0].wait()
    wide = lax.dot_general(
        spread[...], p_v[...], (((1,), (1,)), ((), ())), preferred_element_type=F32
    ).astype(BF16)
    wide = lax.dot_general(
        wide, spread[...], (((1,), (1,)), ((), ())), preferred_element_type=F32
    )
    same = select(wide.shape, lambda r: r & (rows - 1), lambda c: c & (rows - 1))
    kron[...] = (wide * (0.5 * same)).astype(BF16)
    early[1].wait()
    for o in range(chans):
        bias_v[o * rows:(o + 1) * rows, :] = jnp.full((rows, depth), 0.5 * bias_s[o], F32)

    def pointwise(x):
        grid = f_v[:, x].reshape(chans * rows, depth)
        value = jnp.dot(kron[...], grid, preferred_element_type=F32)
        local[x] = value + bias_v[...]

    def stacked(value):
        return jnp.concatenate([value[..., :LANES], value[..., LANES:]], axis=-2)

    table = a_v.reshape(planes * depth, planes * KZ)
    loads[0].wait()
    for h in range(2):
        loads[1 + h].wait()
        grid = jnp.concatenate(
            [f_v[h * half:(h + 1) * half, x].reshape(HALF, depth) for x in range(planes)], axis=1
        )
        turned = jnp.dot(grid, table[...], preferred_element_type=F32).T
        turned = turned.reshape(2, highs * planes, SHARE, HALF)
        part[h] = stacked(turned).astype(BF16)
        if h == 0:
            pl.semaphore_wait(barrier, 1 + len(others))
        pltpu.make_async_remote_copy(
            src_ref=part.at[h, 1 - low],
            dst_ref=got1.at[h],
            send_sem=send1,
            recv_sem=recv1.at[h],
            device_id=(me_y, near),
            device_id_type=MESH,
        ).start()

    for h in range(2):
        arrived(got1.at[h], recv1.at[h])
        owned[h] = (part[h, low].astype(F32) + got1[h].astype(F32)).astype(BF16)
        for d, t, u in others[::-1]:
            pltpu.make_async_remote_copy(
                src_ref=owned.at[h, high_at(u) * planes + flip(mine, d)],
                dst_ref=got2.at[h, high * n_y + me_y],
                send_sem=send2.at[h],
                recv_sem=recv2.at[h],
                device_id=(at(d, t), high_at(u) * 2 + low),
                device_id_type=MESH,
            ).start()
        got2[h, high * n_y + me_y] = owned[h, high * planes + mine]

    for x in range(3):
        pointwise(x)

    for load in loads[3:6]:
        load.wait()
    mode_rows = first_share * SHARE
    most = len(others)
    for h in range(2):
        if h == 1:
            pointwise(3)
        arrived(got2.at[h, 0:most], recv2.at[h])
        pieces = []
        for s in range(n_y):
            total = got2[h, s].astype(F32)
            for u in range(1, highs):
                total += got2[h, u * n_y + s].astype(F32)
            pieces.append(total)
        for j in range(first_share):
            total = pieces[0] * ay_v[j, 0:1, :LANES]
            for s in range(1, n_y):
                total += pieces[s] * ay_v[j, s:s + 1, :LANES]
            u_v[h, j, :, :LANES] = total[:SHARE]
            u_v[h, j, :, LANES:] = total[SHARE:]
        spectrum = jnp.dot(
            u_v[h].reshape(mode_rows, HALF).astype(BF16), e1[...], preferred_element_type=F32
        )
        wide = half * chans
        weights = w_v[:, :, h * wide:(h + 1) * wide].astype(F32).reshape(mode_rows, wide)
        terms = spectrum * weights
        total = terms[:, :LANES]
        for lane in range(LANES, wide, LANES):
            total += terms[:, lane:lane + LANES]
        t_v[...] = total if h == 0 else t_v[...] + total

    landing = modes if group == 1 else got3

    def land(index, sender):
        start = low * highs * planes if group == 1 else 0
        return start + index * n_y + sender

    places = [(d, t) for d in range(planes) for t in range(group)][::-1]
    for g in range(2):
        mixed = jnp.dot(
            t_v[...].astype(BF16), e2[:, g * HALF:(g + 1) * HALF], preferred_element_type=F32
        )
        m_v[g] = mixed.reshape(first_share, SHARE, HALF)
        for index in range(0, len(places), 4):
            batch = places[index:index + 4]
            sums = [None] * len(batch)
            for j in range(first_share):
                mode = m_v[g, j]
                for b, (d, t) in enumerate(batch):
                    term = mode * sy_v[at(d, t), j:j + 1, :]
                    sums[b] = term if j == 0 else sums[b] + term
            for b, (d, t) in enumerate(batch):
                target = at(d, t)
                tout[g, target] = stacked(sums[b]).astype(BF16)
                for u in range(highs):
                    if d == 0 and t == 0 and u == 0:
                        landing[g, land(high, me_y)] = tout[g, target]
                        continue
                    pltpu.make_async_remote_copy(
                        src_ref=tout.at[g, target],
                        dst_ref=landing.at[g, land(high, me_y)],
                        send_sem=send3.at[g],
                        recv_sem=recv3.at[g],
                        device_id=(target, high_at(u) * 2 + low),
                        device_id_type=MESH,
                    ).start()

    for load in loads[6:]:
        load.wait()

    block_of = pl.ds(low * highs * planes, highs * planes)
    for g in range(2):
        for x in range(4 + 2 * g, 6 + 2 * g):
            pointwise(x)
        arrived(landing.at[g, 0:most], recv3.at[g])
        if group > 1:
            for index in range(highs):
                for i in range(planes):
                    total = got3[g, index * n_y + i * group].astype(F32)
                    for t in range(1, group):
                        total += got3[g, index * n_y + i * group + t].astype(F32)
                    modes[g, (low * highs + index) * planes + i] = total.astype(BF16)
        pltpu.make_async_remote_copy(
            src_ref=modes.at[g, block_of],
            dst_ref=modes.at[g, block_of],
            send_sem=send4.at[g],
            recv_sem=recv4.at[g],
            device_id=(me_y, near),
            device_id_type=MESH,
        ).start()

    def turn(g, part_of, start):
        value = modes[g, pl.ds(start, highs * planes)].astype(F32)
        for q in range(2):
            one = value[:, q * SHARE:(q + 1) * SHARE, :].reshape(side, LANES)
            first = g * HALF + q * LANES
            gt_out[first:first + LANES, part_of * side:(part_of + 1) * side] = one.T.astype(BF16)

    for g in range(2):
        turn(g, 0, low * highs * planes)
    for g in range(2):
        arrived(modes.at[g, 0:highs * planes], recv4.at[g])
        turn(g, 1, (1 - low) * highs * planes)
    arrived(got1, send1)
    for g in range(2):
        arrived(got2.at[g, 0:most], send2.at[g])
        arrived(got2.at[g, 0:most], send3.at[g])
        arrived(modes.at[g, 0:highs * planes], send4.at[g])


def grid_kernel(local, gt, synth, out, o_v, out_sem):
    planes, _, depth = local.shape
    chans, _, rows, _ = o_v.shape
    stores = []
    scale = math.sqrt(2.0 / math.pi)
    for x in range(planes):
        value = local[x] + jnp.dot(gt[...], synth[x], preferred_element_type=F32)
        inner = value * (2.0 * scale + (8.0 * scale * 0.044715) * (value * value))
        value += value * jnp.tanh(inner)
        o_v[:, x] = value.astype(BF16).reshape(chans, rows, depth)
        store = pltpu.make_async_copy(o_v.at[:, x], out.at[:, x], out_sem.at[x])
        store.start()
        stores.append(store)
    for store in stores:
        store.wait()


def shards(n_y, n_z, field, spectral_weight, point_weight, bias):
    chans, planes, rows, depth = field.shape
    first_share, depth_share = spectral_weight.shape[:2]
    assert depth_share == SHARE and chans * rows == 2 * HALF and first_share <= KY
    assert n_y % planes == 0 and depth_share * n_z == KZ and planes % 2 == 0 and n_z % 2 == 0
    a_tab, b_tab, ay_tab, sy_tab = tables(n_y, n_z, planes, rows, depth, first_share)
    highs = n_z // 2
    vmem = pl.BlockSpec(memory_space=pltpu.VMEM)
    hbm = pl.BlockSpec(memory_space=pltpu.HBM)
    wide = 2 * HALF
    dma = pltpu.SemaphoreType.DMA
    operands = [field, a_tab, b_tab, spectral_weight, point_weight, bias, ay_tab, sy_tab]
    local, gt, synth = pl.pallas_call(
        functools.partial(spectral_kernel, n_y, n_z),
        out_shape=(
            pltpu.VMEM((planes, wide, depth), F32),
            pltpu.VMEM((wide, planes * KZ), BF16),
            pltpu.VMEM((planes, planes * KZ, depth), BF16),
        ),
        in_specs=[hbm] * len(operands),
        out_specs=(vmem, vmem, vmem),
        scratch_shapes=[
            pltpu.VMEM(field.shape, BF16),
            pltpu.VMEM(a_tab.shape[1:], BF16),
            pltpu.VMEM(spectral_weight.shape, BF16),
            pltpu.VMEM(point_weight.shape, BF16),
            pltpu.SMEM(bias.shape, F32),
            pltpu.VMEM((wide, depth), F32),
            pltpu.VMEM(ay_tab.shape[1:], F32),
            pltpu.VMEM(sy_tab.shape[1:], F32),
            pltpu.VMEM((HALF, chans * chans // 2), BF16),
            pltpu.VMEM((LANES, wide), BF16),
            pltpu.VMEM((wide, chans), BF16),
            pltpu.VMEM((wide, wide), BF16),
            pltpu.VMEM((2, 2, highs * planes, 2 * SHARE, LANES), BF16),
            pltpu.VMEM((2, highs * planes, 2 * SHARE, LANES), BF16),
            pltpu.VMEM((2, highs * planes, 2 * SHARE, LANES), BF16),
            pltpu.VMEM((2, highs * n_y, 2 * SHARE, LANES), BF16),
            pltpu.VMEM((2, first_share, SHARE, HALF), F32),
            pltpu.VMEM((first_share * SHARE, LANES), F32),
            pltpu.VMEM((2, first_share, SHARE, HALF), F32),
            pltpu.VMEM((2, n_y, 2 * SHARE, LANES), BF16),
            pltpu.VMEM((2, highs * n_y, 2 * SHARE, LANES), BF16),
            pltpu.VMEM((2, 2 * highs * planes, 2 * SHARE, LANES), BF16),
            dma((10,)),
            dma(()),
            dma((2,)),
            dma((2,)),
            dma((2,)),
            dma((2,)),
            dma((2,)),
            dma((2,)),
            dma((2,)),
        ],
        compiler_params=pltpu.CompilerParams(
            collective_id=0, has_side_effects=True, vmem_limit_bytes=40 * 1024 * 1024
        ),
        name="spectral",
    )(*(pltpu.with_memory_space_constraint(value, pltpu.HBM) for value in operands))
    return pl.pallas_call(
        grid_kernel,
        out_shape=jax.ShapeDtypeStruct(field.shape, BF16),
        in_specs=[vmem] * 3,
        out_specs=hbm,
        scratch_shapes=[pltpu.VMEM(field.shape, BF16), dma((planes,))],
        compiler_params=pltpu.CompilerParams(vmem_limit_bytes=40 * 1024 * 1024),
        name="grid",
    )(local, gt, synth)


def solution(mesh):
    return jax.shard_map(
        functools.partial(shards, mesh.shape["gy"], mesh.shape["gz"]),
        mesh=mesh,
        in_specs=(P(None, None, "gy", "gz"), P("gy", "gz", None), P(), P()),
        out_specs=P(None, None, "gy", "gz"),
        check_vma=False,
    )
```

```python
import functools
import math

import jax
import jax.numpy as jnp
import ml_dtypes
import numpy as np
from jax import lax
from jax.experimental import pallas as pl
from jax.experimental.pallas import tpu as pltpu
from jax.sharding import PartitionSpec as P

KY = 32
KZ = 32
BF16 = jnp.bfloat16
F32 = jnp.float32
MESH = pl.DeviceIdType.MESH
SHARE = 8
HALF = 256
LANES = 128


def basis(count, length, norm):
    modes = np.arange(count)[:, None]
    spots = np.arange(length)[None, :]
    value = norm * np.cos(np.pi * modes * (spots + 0.5) / length)
    return np.where(modes == 0, value * math.sqrt(0.5), value)


def tables(n_y, n_z, planes, rows, depth, first_share):
    total_rows, total_depth = rows * n_y, depth * n_z
    az = basis(KZ, total_depth, math.sqrt(2.0 / total_depth))
    az = az.astype(np.float32).astype(ml_dtypes.bfloat16).astype(np.float64)
    ax = basis(planes, planes, math.sqrt(2.0 / planes))
    sz = basis(KZ, total_depth, math.sqrt(2.0 / KZ))

    def joint(x_basis, z_basis):
        z = z_basis.reshape(n_z // 2, 2, SHARE, n_z, depth)
        both = np.einsum("ix,hlkdz->dxlhikz", x_basis, z)
        return both.reshape(n_z, planes, planes * KZ, depth).astype(ml_dtypes.bfloat16)

    ay = basis(KY, total_rows, math.sqrt(2.0 / total_rows))
    sy = basis(KY, total_rows, math.sqrt(2.0 / KY))
    blocks = KY // first_share

    def lanes(y_basis):
        parts = y_basis.reshape(blocks, first_share, n_y, rows)
        return np.tile(parts, (1, 1, 1, HALF // rows)).astype(np.float32)

    analysis_y = lanes(ay)
    synth_y = np.ascontiguousarray(np.swapaxes(lanes(0.5 * sy), 1, 2))
    synth = joint(ax, sz).reshape(n_z, planes, 2, planes * KZ // 2, depth)
    analysis = np.ascontiguousarray(np.swapaxes(joint(ax, az), 2, 3))
    return analysis, synth, analysis_y, synth_y


def bits(count):
    assert count & (count - 1) == 0
    return count.bit_length() - 1


def select(shape, row_of, column_of):
    r = row_of(lax.broadcasted_iota(jnp.int32, shape, 0))
    c = column_of(lax.broadcasted_iota(jnp.int32, shape, 1))
    return jnp.where(r == c, 1.0, 0.0).astype(F32)


def spectral_kernel(
    n_y, n_z, field, a_tab, b_tab, weight, point, bias, ay_tab, sy_tab, local, gt_out, b_out,
    f_v, a_v, w_v, p_v, bias_s, bias_v, ay_v, sy_v, e1, e2, spread, kron,
    part, got1, owned, got2, u_v, t_v, m_v, tout, got3, modes,
    load_sem, send1, recv1, send2, recv2, send3, recv3, send4, recv4,
):
    me_y, me_z = lax.axis_index("gy"), lax.axis_index("gz")
    chans, planes, rows, depth = f_v.shape
    group = n_y // planes
    highs = n_z // 2
    high, low = lax.div(me_z, 2), lax.rem(me_z, 2)
    near = high * 2 + 1 - low
    first_share = w_v.shape[0]
    mine, place = lax.div(me_y, group), lax.rem(me_y, group)
    block = place if first_share < KY else 0
    others = [
        (d, t, u) for d in range(planes) for t in range(group) for u in range(highs)
    ][1:]

    def flip(index, mask):
        for k in range(bits(planes)):
            if mask >> k & 1:
                bit = lax.rem(lax.div(index, 1 << k), 2)
                index = index + (1 << k) * (1 - 2 * bit)
        return index

    def at(d, t):
        return flip(mine, d) * group + lax.rem(place + t, group)

    def came(d, t):
        return flip(mine, d) * group + lax.rem(place - t + group, group)

    def high_at(u):
        return lax.rem(high + u, highs)

    def arrived(blocks, semaphore):
        pltpu.make_async_copy(blocks, blocks, semaphore).wait()

    half = chans // 2
    side = planes * KZ // 2
    loads = [
        pltpu.make_async_copy(a_tab.at[me_z], a_v, load_sem.at[0]),
        pltpu.make_async_copy(field.at[0:half], f_v.at[0:half], load_sem.at[1]),
        pltpu.make_async_copy(field.at[half:chans], f_v.at[half:chans], load_sem.at[2]),
        pltpu.make_async_copy(weight, w_v, load_sem.at[3]),
        pltpu.make_async_copy(point, p_v, load_sem.at[4]),
        pltpu.make_async_copy(bias, bias_s, load_sem.at[5]),
        pltpu.make_async_copy(ay_tab.at[block], ay_v, load_sem.at[6]),
        pltpu.make_async_copy(sy_tab.at[block], sy_v, load_sem.at[7]),
        pltpu.make_async_copy(b_tab.at[me_z, :, low], b_out.at[:, 0:side], load_sem.at[8]),
        pltpu.make_async_copy(
            b_tab.at[me_z, :, 1 - low], b_out.at[:, side:2 * side], load_sem.at[9]
        ),
    ]
    for load in loads:
        load.start()

    barrier = pltpu.get_barrier_semaphore()
    pl.semaphore_signal(barrier, inc=1, device_id=(me_y, near), device_id_type=MESH)
    for d, t, u in others:
        pl.semaphore_signal(
            barrier, inc=1, device_id=(at(d, t), high_at(u) * 2 + low), device_id_type=MESH
        )

    e1[...] = select(
        e1.shape, lambda r: r >> bits(rows), lambda c: c >> bits(chans)
    ).astype(BF16)

    def stacked(value):
        return jnp.concatenate([value[..., :LANES], value[..., LANES:]], axis=-2)

    table = a_v.reshape(planes * depth, planes * KZ)
    loads[0].wait()
    for h in range(2):
        loads[1 + h].wait()
        grid = jnp.concatenate(
            [f_v[h * half:(h + 1) * half, x].reshape(HALF, depth) for x in range(planes)], axis=1
        )
        turned = jnp.dot(grid, table[...], preferred_element_type=F32).T
        turned = turned.reshape(2, highs * planes, SHARE, HALF)
        part[h] = stacked(turned).astype(BF16)
        if h == 0:
            pl.semaphore_wait(barrier, 1 + len(others))
        pltpu.make_async_remote_copy(
            src_ref=part.at[h, 1 - low],
            dst_ref=got1.at[h],
            send_sem=send1,
            recv_sem=recv1.at[h],
            device_id=(me_y, near),
            device_id_type=MESH,
        ).start()

    for h in range(2):
        arrived(got1.at[h], recv1.at[h])
        owned[h] = (part[h, low].astype(F32) + got1[h].astype(F32)).astype(BF16)
        for d, t, u in others[::-1]:
            pltpu.make_async_remote_copy(
                src_ref=owned.at[h, high_at(u) * planes + flip(mine, d)],
                dst_ref=got2.at[h, high * n_y + me_y],
                send_sem=send2.at[h],
                recv_sem=recv2.at[h],
                device_id=(at(d, t), high_at(u) * 2 + low),
                device_id_type=MESH,
            ).start()
        got2[h, high * n_y + me_y] = owned[h, high * planes + mine]

    e2[...] = select(
        e2.shape, lambda r: r & (chans - 1), lambda c: c >> bits(rows)
    ).astype(BF16)
    spread[...] = select(spread.shape, lambda r: r >> bits(rows), lambda c: c).astype(BF16)

    loads[4].wait()
    wide = lax.dot_general(
        spread[...], p_v[...], (((1,), (1,)), ((), ())), preferred_element_type=F32
    ).astype(BF16)
    wide = lax.dot_general(
        wide, spread[...], (((1,), (1,)), ((), ())), preferred_element_type=F32
    )
    same = select(wide.shape, lambda r: r & (rows - 1), lambda c: c & (rows - 1))
    kron[...] = (wide * (0.5 * same)).astype(BF16)
    loads[5].wait()
    for o in range(chans):
        bias_v[o * rows:(o + 1) * rows, :] = jnp.full((rows, depth), 0.5 * bias_s[o], F32)

    def pointwise(x):
        grid = f_v[:, x].reshape(chans * rows, depth)
        value = jnp.dot(kron[...], grid, preferred_element_type=F32)
        local[x] = value + bias_v[...]

    for x in range(4):
        pointwise(x)

    for load in (loads[3], loads[6], loads[7]):
        load.wait()
    mode_rows = first_share * SHARE
    most = len(others)
    for h in range(2):
        arrived(got2.at[h, 0:most], recv2.at[h])
        pieces = []
        for s in range(n_y):
            total = got2[h, s].astype(F32)
            for u in range(1, highs):
                total += got2[h, u * n_y + s].astype(F32)
            pieces.append(total)
        for j in range(first_share):
            total = pieces[0] * ay_v[j, 0:1, :LANES]
            for s in range(1, n_y):
                total += pieces[s] * ay_v[j, s:s + 1, :LANES]
            u_v[h, j, :, :LANES] = total[:SHARE]
            u_v[h, j, :, LANES:] = total[SHARE:]
        spectrum = jnp.dot(
            u_v[h].reshape(mode_rows, HALF).astype(BF16), e1[...], preferred_element_type=F32
        )
        wide = half * chans
        weights = w_v[:, :, h * wide:(h + 1) * wide].astype(F32).reshape(mode_rows, wide)
        terms = spectrum * weights
        total = terms[:, :LANES]
        for lane in range(LANES, wide, LANES):
            total += terms[:, lane:lane + LANES]
        t_v[...] = total if h == 0 else t_v[...] + total

    landing = modes if group == 1 else got3

    def land(index, sender):
        start = low * highs * planes if group == 1 else 0
        return start + index * n_y + sender

    places = [(d, t) for d in range(planes) for t in range(group)][::-1]
    for g in range(2):
        mixed = jnp.dot(
            t_v[...].astype(BF16), e2[:, g * HALF:(g + 1) * HALF], preferred_element_type=F32
        )
        m_v[g] = mixed.reshape(first_share, SHARE, HALF)
        for index in range(0, len(places), 4):
            batch = places[index:index + 4]
            sums = [None] * len(batch)
            for j in range(first_share):
                mode = m_v[g, j]
                for b, (d, t) in enumerate(batch):
                    term = mode * sy_v[at(d, t), j:j + 1, :]
                    sums[b] = term if j == 0 else sums[b] + term
            for b, (d, t) in enumerate(batch):
                target = at(d, t)
                tout[g, target] = stacked(sums[b]).astype(BF16)
                for u in range(highs):
                    if d == 0 and t == 0 and u == 0:
                        landing[g, land(high, me_y)] = tout[g, target]
                        continue
                    pltpu.make_async_remote_copy(
                        src_ref=tout.at[g, target],
                        dst_ref=landing.at[g, land(high, me_y)],
                        send_sem=send3.at[g],
                        recv_sem=recv3.at[g],
                        device_id=(target, high_at(u) * 2 + low),
                        device_id_type=MESH,
                    ).start()

    for x in range(4, planes):
        pointwise(x)
    for load in loads[8:]:
        load.wait()

    block_of = pl.ds(low * highs * planes, highs * planes)
    for g in range(2):
        arrived(landing.at[g, 0:most], recv3.at[g])
        if group > 1:
            for index in range(highs):
                for i in range(planes):
                    total = got3[g, index * n_y + i * group].astype(F32)
                    for t in range(1, group):
                        total += got3[g, index * n_y + i * group + t].astype(F32)
                    modes[g, (low * highs + index) * planes + i] = total.astype(BF16)
        pltpu.make_async_remote_copy(
            src_ref=modes.at[g, block_of],
            dst_ref=modes.at[g, block_of],
            send_sem=send4.at[g],
            recv_sem=recv4.at[g],
            device_id=(me_y, near),
            device_id_type=MESH,
        ).start()

    def turn(g, part_of, start):
        value = modes[g, pl.ds(start, highs * planes)].astype(F32)
        for q in range(2):
            one = value[:, q * SHARE:(q + 1) * SHARE, :].reshape(side, LANES)
            first = g * HALF + q * LANES
            gt_out[first:first + LANES, part_of * side:(part_of + 1) * side] = one.T.astype(BF16)

    for g in range(2):
        turn(g, 0, low * highs * planes)
    for g in range(2):
        arrived(modes.at[g, 0:highs * planes], recv4.at[g])
        turn(g, 1, (1 - low) * highs * planes)
    arrived(got1, send1)
    for g in range(2):
        arrived(got2.at[g, 0:most], send2.at[g])
        arrived(got2.at[g, 0:most], send3.at[g])
        arrived(modes.at[g, 0:highs * planes], send4.at[g])


def grid_kernel(local, gt, synth, out, o_v, out_sem):
    planes, _, depth = local.shape
    chans, _, rows, _ = o_v.shape
    stores = []
    scale = math.sqrt(2.0 / math.pi)
    for x in range(planes):
        value = local[x] + jnp.dot(gt[...], synth[x], preferred_element_type=F32)
        inner = value * (2.0 * scale + (8.0 * scale * 0.044715) * (value * value))
        value += value * jnp.tanh(inner)
        o_v[:, x] = value.astype(BF16).reshape(chans, rows, depth)
        store = pltpu.make_async_copy(o_v.at[:, x], out.at[:, x], out_sem.at[x])
        store.start()
        stores.append(store)
    for store in stores:
        store.wait()


def shards(n_y, n_z, field, spectral_weight, point_weight, bias):
    chans, planes, rows, depth = field.shape
    first_share, depth_share = spectral_weight.shape[:2]
    assert depth_share == SHARE and chans * rows == 2 * HALF and first_share <= KY
    assert n_y % planes == 0 and depth_share * n_z == KZ and planes % 2 == 0 and n_z % 2 == 0
    a_tab, b_tab, ay_tab, sy_tab = tables(n_y, n_z, planes, rows, depth, first_share)
    highs = n_z // 2
    vmem = pl.BlockSpec(memory_space=pltpu.VMEM)
    hbm = pl.BlockSpec(memory_space=pltpu.HBM)
    wide = 2 * HALF
    dma = pltpu.SemaphoreType.DMA
    operands = [field, a_tab, b_tab, spectral_weight, point_weight, bias, ay_tab, sy_tab]
    local, gt, synth = pl.pallas_call(
        functools.partial(spectral_kernel, n_y, n_z),
        out_shape=(
            pltpu.VMEM((planes, wide, depth), F32),
            pltpu.VMEM((wide, planes * KZ), BF16),
            pltpu.VMEM((planes, planes * KZ, depth), BF16),
        ),
        in_specs=[hbm] * len(operands),
        out_specs=(vmem, vmem, vmem),
        scratch_shapes=[
            pltpu.VMEM(field.shape, BF16),
            pltpu.VMEM(a_tab.shape[1:], BF16),
            pltpu.VMEM(spectral_weight.shape, BF16),
            pltpu.VMEM(point_weight.shape, BF16),
            pltpu.SMEM(bias.shape, F32),
            pltpu.VMEM((wide, depth), F32),
            pltpu.VMEM(ay_tab.shape[1:], F32),
            pltpu.VMEM(sy_tab.shape[1:], F32),
            pltpu.VMEM((HALF, chans * chans // 2), BF16),
            pltpu.VMEM((LANES, wide), BF16),
            pltpu.VMEM((wide, chans), BF16),
            pltpu.VMEM((wide, wide), BF16),
            pltpu.VMEM((2, 2, highs * planes, 2 * SHARE, LANES), BF16),
            pltpu.VMEM((2, highs * planes, 2 * SHARE, LANES), BF16),
            pltpu.VMEM((2, highs * planes, 2 * SHARE, LANES), BF16),
            pltpu.VMEM((2, highs * n_y, 2 * SHARE, LANES), BF16),
            pltpu.VMEM((2, first_share, SHARE, HALF), F32),
            pltpu.VMEM((first_share * SHARE, LANES), F32),
            pltpu.VMEM((2, first_share, SHARE, HALF), F32),
            pltpu.VMEM((2, n_y, 2 * SHARE, LANES), BF16),
            pltpu.VMEM((2, highs * n_y, 2 * SHARE, LANES), BF16),
            pltpu.VMEM((2, 2 * highs * planes, 2 * SHARE, LANES), BF16),
            dma((10,)),
            dma(()),
            dma((2,)),
            dma((2,)),
            dma((2,)),
            dma((2,)),
            dma((2,)),
            dma((2,)),
            dma((2,)),
        ],
        compiler_params=pltpu.CompilerParams(
            collective_id=0, has_side_effects=True, vmem_limit_bytes=40 * 1024 * 1024
        ),
        name="spectral",
    )(*(pltpu.with_memory_space_constraint(value, pltpu.HBM) for value in operands))
    return pl.pallas_call(
        grid_kernel,
        out_shape=jax.ShapeDtypeStruct(field.shape, BF16),
        in_specs=[vmem] * 3,
        out_specs=hbm,
        scratch_shapes=[pltpu.VMEM(field.shape, BF16), dma((planes,))],
        compiler_params=pltpu.CompilerParams(vmem_limit_bytes=40 * 1024 * 1024),
        name="grid",
    )(local, gt, synth)


def solution(mesh):
    return jax.shard_map(
        functools.partial(shards, mesh.shape["gy"], mesh.shape["gz"]),
        mesh=mesh,
        in_specs=(P(None, None, "gy", "gz"), P("gy", "gz", None), P(), P()),
        out_specs=P(None, None, "gy", "gz"),
        check_vma=False,
    )
```
